128 devices in a mesh: ctx: 16 (over y, z_hi, core), tp: 8 (over x, z_lo).
Axes of the slice: x: 4, y: 4, z: 4 (z_hi: 2, z_lo: 2; z = z_hi * 2 + z_lo), core: 2. Of those that a mesh axis runs over, the one named last changes fastest.
Arguments:
- query: bfloat16 [2048, 64, 576], P('ctx', 'tp')
- latent: bfloat16 [2048, 576], P('ctx')
- d_out: bfloat16 [2048, 64, 512], P('ctx', 'tp'), may hold values from -1.5 to 1.5
- positions: int32 [2048], P('ctx'), may hold values from 0 to 2047, as said below
- doc_ids: int32 [2048], replicated, may hold values from 0 to 3, never falling along the last dimension, each value on 1 to 1024 neighbouring positions
Outputs:
- d_query: bfloat16 [2048, 64, 576], P('ctx', 'tp')
- d_latent: bfloat16 [2048, 576], P('ctx')
The draws below stay inside these ranges and needn't reach their ends.
Inputs may be any that keep to these rules, and one draw needn't show every extreme that they name: A permutation; the rows of each index d of ctx hold two runs of 64 consecutive increasing positions: run b and the mirrored run counted from the end, b differing between indices.
All inputs are finite; a program needn't handle non-finite values.
Results may differ from the reference program's by a relative error of at most 0.024.
Values may be sent and summed in bfloat16 or wider, within the bound.
A program may use at most 128 MiB of HBM per device.

```python
import math
import jax
import jax.numpy as jnp
import numpy as np
from jax import lax

TOK_DEV = 128
LAT = 512
ROPE = 64
TOKENS = 2048
HEADS = 64
N_CTX = 16


def shared_latent(key):
    return jax.random.normal(key, (TOKENS, LAT + ROPE), jnp.float32)


def draw_latent(key, part):
    base = shared_latent(key)
    return base.astype(jnp.bfloat16)


def draw_query(key, part):
    key = jax.random.fold_in(key, 23)
    values = jax.random.normal(key, (TOKENS, HEADS, LAT + ROPE), jnp.float32)
    return values.astype(jnp.bfloat16)


def draw_positions(key, part):
    key = jax.random.fold_in(key, 5)
    order = jax.random.permutation(key, N_CTX)
    half = TOK_DEV // 2
    index = jnp.arange(TOKENS, dtype=jnp.int32)
    device = index // TOK_DEV
    within = index % TOK_DEV
    lower = order[device]
    block = jnp.where(within < half, lower, 2 * N_CTX - 1 - lower)
    return (block * half + within % half).astype(jnp.int32)


def levels(own_key, shape, cuts, low, high):
    level, own = 1.0, jax.random.fold_in(own_key, 6)
    for dim, shards_of in cuts:
        heights = jnp.exp(jax.random.uniform(jax.random.fold_in(own, dim), (shards_of,), jnp.float32, low / len(cuts), high / len(cuts)))
        level = level * jnp.repeat(heights, shape[dim] // shards_of).reshape([-1 if axis == dim else 1 for axis in range(len(shape))])
    return level


def profile(number_of, total, bound, skew):
    loads = [(1 << 20) // math.isqrt(grade ** skew) + 1 for grade in range(2, number_of + 1)]
    rest, counts = total - bound - (number_of - 1), [1] * (number_of - 1)
    while rest > 0:
        movable = [i for i in range(number_of - 1) if counts[i] < bound]
        pool, left = sum([loads[i] for i in movable]), rest
        for i in movable:
            extra = min(bound - counts[i], max(1, left * loads[i] // pool), rest)
            counts[i] = counts[i] + extra
            rest = rest - extra
    return np.array([bound] + counts)


def uneven_parts(key, amount, total, limit, lean):
    if amount == 2:
        one = jax.random.randint(key, (), max(1, total - limit), min(limit, total - 1) + 1)
        return jnp.stack([one, total - one])
    tallies = jnp.asarray(profile(amount, total, limit, lean), jnp.int32)
    twos = (amount - 1) // 2
    giver, sink = tallies[1:1 + 2 * twos:2], tallies[2:2 + 2 * twos:2]
    slack = jnp.minimum(giver - 1, limit - sink)
    shifted = jax.random.randint(jax.random.fold_in(key, 1), (twos,), 0, 1 << 20) % (slack + 1)
    tallies = tallies.at[1:1 + 2 * twos:2].set(giver - shifted).at[2:2 + 2 * twos:2].set(sink + shifted)
    return tallies[jax.random.permutation(jax.random.fold_in(key, 2), amount)]


def bell_draw(own_key, shape, scale, bound, cuts=(), kind=jnp.bfloat16):
    loudness = levels(own_key, shape, cuts, -0.22, 0.18) if cuts else 1.0
    entries = jax.random.normal(own_key, shape, jnp.float32) * scale * loudness
    return jnp.minimum(jnp.maximum(entries, -bound), bound).astype(kind)


def setup_inputs(seed: int = 0) -> dict:
    key_list = jax.random.split(jax.random.key(seed), 6)
    query = draw_query(jax.random.fold_in(key_list[5], 71), 0)
    latent = draw_latent(jax.random.fold_in(key_list[5], 71), 0)
    d_out = bell_draw(key_list[2], (TOKENS, HEADS, LAT), 0.25, 1.5, ((0, 16), (1, 8)))
    positions = draw_positions(jax.random.fold_in(key_list[5], 71), 0)
    doc_ids = jnp.searchsorted(jnp.cumsum(uneven_parts(key_list[4], 4, TOKENS, TOKENS // 2, 2)), jnp.arange(TOKENS), side="right").astype(jnp.int32)
    return {"query": query, "latent": latent, "d_out": d_out, "positions": positions, "doc_ids": doc_ids}


SCALE = 192.0 ** -0.5


def reference(query, latent, d_out, positions, doc_ids):
    docs = doc_ids[positions]
    allowed = (positions[None, :] <= positions[:, None]) & (docs[None, :] == docs[:, None])
    values = latent[:, :LAT]
    width = LAT + ROPE

    def head_step(total, index):
        qrow = lax.dynamic_index_in_dim(query, index, 1, keepdims=False)
        grow = lax.dynamic_index_in_dim(d_out, index, 1, keepdims=False)
        score = SCALE * lax.dot_general(qrow, latent, (((1,), (1,)), ((), ())), preferred_element_type=jnp.float32)
        masked = jnp.where(allowed, score, jnp.float32(-1e30))
        peak = jnp.max(masked, axis=1)
        expo = jnp.where(allowed, jnp.exp(masked - peak[:, None]), jnp.float32(0.0))
        denom = jnp.sum(expo, axis=1)
        out = (jnp.dot(expo.astype(jnp.bfloat16), values, preferred_element_type=jnp.float32) / denom[:, None]).astype(jnp.bfloat16)
        lse = peak + jnp.log(denom)
        delta = jnp.sum(grow.astype(jnp.float32) * out.astype(jnp.float32), axis=1)
        prob = jnp.exp(jnp.where(allowed, score - lse[:, None], jnp.float32(-1e30)))
        grad_p = lax.dot_general(grow, values, (((1,), (1,)), ((), ())), preferred_element_type=jnp.float32)
        grad_s = (prob * (grad_p - delta[:, None])).astype(jnp.bfloat16)
        dq = (SCALE * jnp.dot(grad_s, latent, preferred_element_type=jnp.float32)).astype(jnp.bfloat16)
        dk = SCALE * lax.dot_general(grad_s, qrow, (((0,), (0,)), ((), ())), preferred_element_type=jnp.float32)
        dv = lax.dot_general(prob.astype(jnp.bfloat16), grow, (((0,), (0,)), ((), ())), preferred_element_type=jnp.float32)
        dk = dk + jnp.pad(dv, ((0, 0), (0, width - LAT)))
        return total + dk, dq

    start = jnp.zeros((query.shape[0], width), jnp.float32)
    total, dqs = lax.scan(head_step, start, jnp.arange(query.shape[1], dtype=jnp.int32))
    return jnp.transpose(dqs, (1, 0, 2)), total.astype(jnp.bfloat16)
```

```python
import functools

import jax
import jax.numpy as jnp
from jax import lax
from jax.experimental import pallas as pl
from jax.experimental.pallas import tpu as pltpu
from jax.sharding import PartitionSpec as P

MESH = pl.DeviceIdType.MESH
F32, BF16, I32 = jnp.float32, jnp.bfloat16, jnp.int32
SCALE = 192.0 ** (-0.5)
LOG2E = 1.4426950408889634
WIDTH, LAT, TOK, HEADS, RUN = 576, 512, 128, 8, 64
ROWS = HEADS * RUN
N_CTX, N_TP, N_DOCS = 16, 8, 4
TILES = N_CTX + 1
BLOCKS = 5
PIECE = 80


def dot(left, right):
    return jnp.dot(left, right, preferred_element_type=F32)


def dot_nt(left, right):
    return lax.dot_general(left, right, (((1,), (1,)), ((), ())), preferred_element_type=F32)


def remote(src, dst, send, recv, device):
    return pltpu.make_async_remote_copy(
        src_ref=src, dst_ref=dst, send_sem=send, recv_sem=recv, device_id=device, device_id_type=MESH
    )


def greet(devices):
    barrier = pltpu.get_barrier_semaphore()
    for device in devices:
        pl.semaphore_signal(barrier, inc=1, device_id=device, device_id_type=MESH)
    pl.semaphore_wait(barrier, len(devices))


def gather_kernel(
    latent, positions, docs, query, d_out,
    all_latent, all_positions, starts, q_rows, q_cols, g_rows, g_cols,
    q_in, g_in, g_wide, own_sem, in_sem, send_sem, recv_sem, core_send, core_recv, pos_send, pos_recv,
):
    ctx, tp = lax.axis_index("ctx"), lax.axis_index("tp")
    core, group = lax.rem(ctx, 2), ctx // 2
    twin = (2 * group + 1 - core, tp)
    load_q = pltpu.make_async_copy(query, q_in, in_sem.at[0])
    load_g = pltpu.make_async_copy(d_out, g_in, in_sem.at[1])
    load_q.start()
    load_g.start()
    own = [
        pltpu.make_async_copy(latent, all_latent.at[ctx], own_sem.at[0]),
        pltpu.make_async_copy(positions, all_positions.at[ctx], own_sem.at[1]),
    ]
    for copy in own:
        copy.start()
    same = [(2 * lax.rem(group + k, 8) + core, tp) for k in range(1, 8)]
    every = [(lax.rem(ctx + k, N_CTX), tp) for k in range(1, N_CTX)]
    greet(every)
    sends = []
    for k, device in enumerate(same):
        sends.append(remote(latent, all_latent.at[ctx], send_sem.at[k], recv_sem.at[k], device))
    sends.append(remote(latent, all_latent.at[ctx], core_send.at[7], core_recv.at[7], twin))
    small = []
    for k, device in enumerate(every):
        small.append(remote(positions, all_positions.at[ctx], pos_send.at[k], pos_recv.at[k], device))
    for copy in sends + small:
        copy.start()

    counts = [jnp.sum((docs[...] < value).astype(I32), keepdims=True) for value in range(1, N_DOCS)]
    row = lax.broadcasted_iota(I32, (8, TOK), 0)
    table = jnp.zeros((8, TOK), I32)
    for index, count in enumerate(counts):
        table = jnp.where(row == index, count, table)
    starts[...] = table

    load_q.wait()
    for h in range(HEADS):
        columns = q_in[h]
        rows = columns.T
        for run in range(2):
            q_rows[run, RUN * h : RUN * (h + 1), :] = rows[RUN * run : RUN * (run + 1)]
    for run in range(2):
        for part in range(ROWS // 128):
            pair = slice(128 * part, 128 * (part + 1))
            q_cols[run, :, pair] = q_rows[run, pair, :].T
    load_g.wait()
    for part in range(LAT // 128):
        lanes = slice(128 * part, 128 * (part + 1))
        g_wide[part] = g_in[:, lanes].astype(F32)
        for h in range(HEADS):
            rows = g_wide[part, pl.ds(h, TOK, HEADS), :].astype(BF16)
            for run in range(2):
                g_rows[run, RUN * h : RUN * (h + 1), lanes] = rows[RUN * run : RUN * (run + 1)]
    for run in range(2):
        for part in range(ROWS // 128):
            pair = slice(128 * part, 128 * (part + 1))
            g_cols[run, :, pair] = g_rows[run, pair, :].T

    forwards = []
    for k in range(7):
        slot = 2 * lax.rem(group + 8 - (k + 1), 8) + core
        block = all_latent.at[slot]
        sends[k].wait_send()
        remote(latent, block, send_sem.at[k], recv_sem.at[k], same[k]).wait_recv()
        forward = remote(block, block, core_send.at[k], core_recv.at[k], twin)
        forward.start()
        forwards.append(forward)
    for copy in forwards + sends[7:] + small:
        copy.wait()
    for copy in own:
        copy.wait()


def gather(latent, positions, docs, query, d_out):
    whole, fast = pl.BlockSpec(memory_space=pl.ANY), pl.BlockSpec(memory_space=pltpu.VMEM)
    return pl.pallas_call(
        gather_kernel,
        out_shape=[
            jax.ShapeDtypeStruct((N_CTX, WIDTH, TOK), BF16),
            jax.ShapeDtypeStruct((N_CTX, 1, TOK), I32),
            jax.ShapeDtypeStruct((8, TOK), I32),
            jax.ShapeDtypeStruct((2, ROWS, WIDTH), BF16),
            jax.ShapeDtypeStruct((2, WIDTH, ROWS), BF16),
            jax.ShapeDtypeStruct((2, ROWS, LAT), BF16),
            jax.ShapeDtypeStruct((2, LAT, ROWS), BF16),
        ],
        in_specs=[whole, whole, fast, whole, whole],
        out_specs=[whole, whole] + [fast] * 5,
        scratch_shapes=[
            pltpu.VMEM((HEADS, WIDTH, TOK), BF16),
            pltpu.VMEM((TOK * HEADS, LAT), BF16),
            pltpu.VMEM((LAT // 128, TOK * HEADS, 128), F32),
            pltpu.SemaphoreType.DMA((2,)),
            pltpu.SemaphoreType.DMA((2,)),
            pltpu.SemaphoreType.DMA((7,)),
            pltpu.SemaphoreType.DMA((7,)),
            pltpu.SemaphoreType.DMA((8,)),
            pltpu.SemaphoreType.DMA((8,)),
            pltpu.SemaphoreType.DMA((15,)),
            pltpu.SemaphoreType.DMA((15,)),
        ],
        compiler_params=pltpu.CompilerParams(
            collective_id=0, has_side_effects=True, vmem_limit_bytes=48 << 20
        ),
        name="gather",
    )(latent, positions, docs, query, d_out)


def attention_kernel(
    places, starts, mine, latent, q_rows, q_cols, g_rows, g_cols,
    d_query, partial,
    where_is, keys, score, grad_p, dq, dkv,
):
    for device in range(N_CTX):
        for half in range(2):
            where_is[places[device, 0, RUN * half] // RUN] = 2 * device + half
    low = lax.broadcasted_iota(I32, (WIDTH, TOK), 1) < RUN
    keys[0] = jnp.zeros((WIDTH, TOK), BF16)
    dkv[...] = jnp.zeros_like(dkv)

    def halves(first, second, first_half, second_half):
        first = jnp.where(first_half == 0, first, pltpu.roll(first, RUN, 1))
        second = jnp.where(second_half == 1, second, pltpu.roll(second, RUN, 1))
        return jnp.where(low, first, second)

    def sort(tile, carry):
        one, two = where_is[2 * tile], where_is[2 * tile + 1]
        keys[tile + 1] = halves(
            latent[one // 2].astype(F32), latent[two // 2].astype(F32), one % 2, two % 2
        ).astype(BF16)
        return carry

    lax.fori_loop(0, N_CTX, sort, 0)
    bounds = [starts[index, 0] for index in range(N_DOCS - 1)]

    for run in range(2):
        base = mine[0, RUN * run]
        position = base + lax.broadcasted_iota(I32, (ROWS, 1), 0) % RUN
        begin = jnp.zeros((ROWS, 1), I32)
        oldest = jnp.int32(0)
        for bound in bounds:
            begin = jnp.where(position >= bound, bound, begin)
            oldest = jnp.where(base >= bound, bound, oldest)
        last = base // TOK + 2
        count = (last - 1 - oldest // TOK + 1) // 2

        def block_of(index):
            first = last - 2 * (index + 1)
            return first, jnp.concatenate([keys[first], keys[first + 1]], axis=1)

        def scores(index, peak):
            first, block = block_of(index)
            at = (first - 1) * TOK + lax.broadcasted_iota(I32, (ROWS, 2 * TOK), 1)
            allowed = (at <= position) & (at >= begin)
            value = jnp.where(allowed, dot(q_rows[run], block) * (SCALE * LOG2E), -1e30)
            score[index] = value
            grad_p[index] = dot(g_rows[run], block[:LAT])
            return jnp.maximum(peak, jnp.maximum(value[:, :TOK], value[:, TOK:]))

        peak = lax.fori_loop(0, count, scores, jnp.full((ROWS, TOK), -1e30, F32))
        peak = jnp.max(peak, axis=1, keepdims=True)

        def sums(index, carry):
            total, mixed = carry
            weight = jnp.exp2(score[index] - peak)
            score[index] = weight
            product = weight * grad_p[index]
            return (
                total + weight[:, :TOK] + weight[:, TOK:],
                mixed + product[:, :TOK] + product[:, TOK:],
            )

        zero = jnp.zeros((ROWS, TOK), F32)
        total, mixed = lax.fori_loop(0, count, sums, (zero, zero))
        inverse = 1.0 / jnp.sum(total, axis=1, keepdims=True)
        delta = jnp.sum(mixed, axis=1, keepdims=True) * inverse
        dq[run] = jnp.zeros((ROWS, WIDTH), F32)

        def grads(index, carry):
            first, block = block_of(index)
            prob = score[index] * inverse
            grad_s = (prob * (grad_p[index] - delta) * SCALE).astype(BF16)
            dq[run] += dot_nt(grad_s, block)
            d_keys = dot(q_cols[run], grad_s)
            d_values = dot(g_cols[run], prob.astype(BF16))
            for half in range(2):
                columns = slice(TOK * half, TOK * (half + 1))
                dkv[first + half, :LAT] += d_keys[:LAT, columns] + d_values[:, columns]
                dkv[first + half, LAT:] += d_keys[LAT:, columns]
            return carry

        lax.fori_loop(0, count, grads, 0)

    for h in range(HEADS):
        rows = slice(RUN * h, RUN * (h + 1))
        both = jnp.concatenate([dq[0, rows, :], dq[1, rows, :]], axis=0)
        d_query[h] = both.T.astype(BF16)

    def unsort(device, carry):
        one, two = places[device, 0, 0] // RUN, places[device, 0, RUN] // RUN
        owner = device // 2 + 8 * (device % 2)
        partial[owner] = halves(
            dkv[one // 2 + 1], dkv[two // 2 + 1], one % 2, two % 2
        ).astype(BF16)
        return carry

    lax.fori_loop(0, N_CTX, unsort, 0)


def attention(places, starts, mine, latent, q_rows, q_cols, g_rows, g_cols):
    fast, scalar = pl.BlockSpec(memory_space=pltpu.VMEM), pl.BlockSpec(memory_space=pltpu.SMEM)
    return pl.pallas_call(
        attention_kernel,
        out_shape=[
            jax.ShapeDtypeStruct((HEADS, WIDTH, TOK), BF16),
            jax.ShapeDtypeStruct((N_CTX, WIDTH, TOK), BF16),
        ],
        in_specs=[scalar] * 3 + [fast] * 5,
        out_specs=[fast, fast],
        scratch_shapes=[
            pltpu.SMEM((2 * N_CTX,), I32),
            pltpu.VMEM((TILES, WIDTH, TOK), BF16),
            pltpu.VMEM((BLOCKS, ROWS, 2 * TOK), F32),
            pltpu.VMEM((BLOCKS, ROWS, 2 * TOK), F32),
            pltpu.VMEM((2, ROWS, WIDTH), F32),
            pltpu.VMEM((TILES, WIDTH, TOK), F32),
        ],
        compiler_params=pltpu.CompilerParams(vmem_limit_bytes=56 << 20),
        name="attention",
    )(places, starts, mine, latent, q_rows, q_cols, g_rows, g_cols)


def total_kernel(
    partial, result,
    half, twin_part, chip, group_part, ours, piece_part, piece, final_part,
    in_sem, core_send, core_recv, ctx_send, ctx_recv, tp_send, tp_recv, out_send, out_recv,
):
    ctx, tp = lax.axis_index("ctx"), lax.axis_index("tp")
    core, group = lax.rem(ctx, 2), ctx // 2
    twin = (2 * group + 1 - core, tp)
    same = [(2 * lax.rem(group + k, 8) + core, tp) for k in range(1, 8)]
    heads = [(ctx, lax.rem(tp + k, N_TP)) for k in range(1, N_TP)]

    def rows_of(index):
        return pl.ds(pl.multiple_of(144 * (index // 2) + 64 * lax.rem(index, 2), 16), PIECE)

    load = pltpu.make_async_copy(partial.at[pl.ds(8 * core, 8)], half, in_sem)
    load.start()
    greet([twin] + same + heads)
    to_twin = []
    for k in range(8):
        owner = lax.rem(group + k, 8)
        copy = remote(
            partial.at[8 * (1 - core) + owner], twin_part.at[k], core_send.at[k], core_recv.at[k], twin
        )
        copy.start()
        to_twin.append(copy)
    load.wait()
    to_group = []
    for k in list(range(1, 8)) + [0]:
        owner = lax.rem(group + k, 8)
        to_twin[k].wait_recv()
        both = half[owner].astype(F32) + twin_part[k].astype(F32)
        if k:
            chip[k - 1] = both.astype(BF16)
            copy = remote(
                chip.at[k - 1], group_part.at[k - 1], ctx_send.at[k - 1], ctx_recv.at[k - 1], same[k - 1]
            )
            copy.start()
            to_group.append(copy)
        else:
            mine = both
    for copy in to_group:
        copy.wait_recv()
    for k in range(7):
        mine = mine + group_part[k].astype(F32)
    ours[...] = mine.astype(BF16)
    to_heads = []
    for k in range(7):
        rows = rows_of(lax.rem(tp + k + 1, N_TP))
        copy = remote(ours.at[rows], piece_part.at[k], tp_send.at[k], tp_recv.at[k], heads[k])
        copy.start()
        to_heads.append(copy)
    mine = ours[rows_of(tp), :].astype(F32)
    for copy in to_heads:
        copy.wait_recv()
    for k in range(7):
        mine = mine + piece_part[k].astype(F32)
    piece[...] = mine.astype(BF16)
    to_all = []
    for k in range(7):
        copy = remote(piece, final_part.at[k], out_send.at[k], out_recv.at[k], heads[k])
        copy.start()
        to_all.append(copy)
    result[rows_of(tp), :] = piece[...]
    for k in range(7):
        to_all[k].wait_recv()
        result[rows_of(lax.rem(tp + 7 - k, N_TP)), :] = final_part[k]
    for copy in to_twin + to_group + to_heads + to_all:
        copy.wait_send()


def total(partial):
    dma = pltpu.SemaphoreType.DMA
    return pl.pallas_call(
        total_kernel,
        out_shape=jax.ShapeDtypeStruct((WIDTH, TOK), BF16),
        in_specs=[pl.BlockSpec(memory_space=pl.ANY)],
        out_specs=pl.BlockSpec(memory_space=pltpu.VMEM),
        scratch_shapes=[
            pltpu.VMEM((8, WIDTH, TOK), BF16),
            pltpu.VMEM((8, WIDTH, TOK), BF16),
            pltpu.VMEM((7, WIDTH, TOK), BF16),
            pltpu.VMEM((7, WIDTH, TOK), BF16),
            pltpu.VMEM((WIDTH, TOK), BF16),
            pltpu.VMEM((7, PIECE, TOK), BF16),
            pltpu.VMEM((PIECE, TOK), BF16),
            pltpu.VMEM((7, PIECE, TOK), BF16),
            dma,
            dma((8,)),
            dma((8,)),
            dma((7,)),
            dma((7,)),
            dma((7,)),
            dma((7,)),
            dma((7,)),
            dma((7,)),
        ],
        compiler_params=pltpu.CompilerParams(
            collective_id=1, has_side_effects=True, vmem_limit_bytes=48 << 20
        ),
        name="total",
    )(partial)


def local(query, latent, d_out, positions, doc_ids):
    here = positions.reshape(1, TOK)
    columns, places, starts, q_rows, q_cols, g_rows, g_cols = gather(
        latent.T,
        here,
        doc_ids.reshape(-1, TOK),
        query.transpose(1, 2, 0),
        d_out.reshape(TOK * HEADS, LAT),
    )
    d_query, partial = attention(places, starts, here, columns, q_rows, q_cols, g_rows, g_cols)
    d_latent = total(partial)
    return (d_query.transpose(2, 0, 1), d_latent.T)


def solution(mesh):
    return jax.shard_map(
        local,
        mesh=mesh,
        in_specs=(P("ctx", "tp", None), P("ctx", None), P("ctx", "tp", None), P("ctx"), P()),
        out_specs=(P("ctx", "tp", None), P("ctx", None)),
        check_vma=False,
    )
```

```python
import jax
import jax.numpy as jnp
from jax import lax
from jax.experimental import pallas as pl
from jax.experimental.pallas import tpu as pltpu
from jax.sharding import PartitionSpec as P

MESH = pl.DeviceIdType.MESH
F32, BF16, I32 = jnp.float32, jnp.bfloat16, jnp.int32
SCALE = 192.0 ** (-0.5)
LOG2E = 1.4426950408889634
WIDTH, LAT, TOK, HEADS, RUN = 576, 512, 128, 8, 64
ROWS = HEADS * RUN
N_CTX, N_TP, N_DOCS = 16, 8, 4
SLOTS = 9
SPAN = SLOTS * TOK
QUARTER = WIDTH // 4
X_PIECE, Y_PIECE = 80, 64
X_ROWS, Y_ROWS = 4 * X_PIECE, 4 * Y_PIECE
INVERSE, STARTS = N_CTX, N_CTX + 1


def dot(left, right):
    return jnp.dot(left, right, preferred_element_type=F32)


def dot_nt(left, right):
    return lax.dot_general(left, right, (((1,), (1,)), ((), ())), preferred_element_type=F32)


def remote(src, dst, send, recv, device):
    return pltpu.make_async_remote_copy(
        src_ref=src, dst_ref=dst, send_sem=send, recv_sem=recv, device_id=device, device_id_type=MESH
    )


def greet(devices):
    barrier = pltpu.get_barrier_semaphore()
    for device in devices:
        pl.semaphore_signal(barrier, inc=1, device_id=device, device_id_type=MESH)
    pl.semaphore_wait(barrier, len(devices))


def kernel(
    latent, positions, docs, query, d_out, d_query, d_latent,
    q_in, g_in, g_wide, q_rows, q_cols, g_rows, g_cols, blocks, places, info, table,
    keys, score, grad_p, prob, grad_s, dkv, dq,
    x_part, y_part, x_twin, y_twin, x_chip, y_chip, x_recv, y_recv, x_sum, y_sum,
    x_last, y_last, piece, pieces,
    in_sem, info_sem, a_send, a_recv, b_send, b_recv, c_send, c_recv, pos_send, pos_recv,
    t_send, t_recv, x_send, x_got, y_send, y_got, xl_send, xl_got, yl_send, yl_got, o_send, o_recv,
):
    ctx, tp = lax.axis_index("ctx"), lax.axis_index("tp")
    core, group = lax.rem(ctx, 2), ctx // 2
    x, low_z = tp // 2, lax.rem(tp, 2)

    def turn(index, step, size):
        return lax.rem(index + step + size, size)

    def along_x(step):
        return (ctx, 2 * turn(x, step, 4) + low_z)

    twin = (2 * group + 1 - core, tp)
    same = [(2 * turn(group, k, 8) + core, tp) for k in range(1, 8)]
    every = [(turn(ctx, k, N_CTX), tp) for k in range(1, N_CTX)]
    over_tp = [(ctx, turn(tp, k, N_TP)) for k in range(1, N_TP)]
    plane = [
        (2 * turn(group, k, 8) + core, 2 * x + turn(low_z, j, 2))
        for j in range(2) for k in range(8) if j or k
    ]

    loads = [
        pltpu.make_async_copy(latent, blocks.at[ctx], in_sem.at[0]),
        pltpu.make_async_copy(query, q_in, in_sem.at[1]),
        pltpu.make_async_copy(d_out, g_in, in_sem.at[2]),
    ]
    for copy in loads:
        copy.start()
    places[ctx] = positions[...]
    greet(every + over_tp + plane[7:][1:])

    def quarter(index):
        return pl.ds(pl.multiple_of(QUARTER * index, 16), QUARTER)

    small = []
    for k, device in enumerate(every):
        mine = places.at[ctx]
        small.append(remote(mine, mine, pos_send.at[k], pos_recv.at[k], device))
    for copy in small:
        copy.start()
    loads[0].wait()
    first = []
    for k, device in enumerate(same):
        for j in range(2):
            part = blocks.at[ctx, quarter(turn(x, j, 4))]
            copy = remote(part, part, a_send.at[2 * k + j], a_recv.at[2 * k + j], device)
            copy.start()
            first.append(copy)
    to_twin = [remote(blocks.at[ctx], blocks.at[ctx], c_send.at[7], c_recv.at[7], twin)]
    to_twin[0].start()

    loads[1].wait()
    for h in range(HEADS):
        rows = q_in[h].T
        for run in range(2):
            q_rows[run, RUN * h : RUN * (h + 1), :] = rows[RUN * run : RUN * (run + 1)]

    def sender(k):
        return 2 * turn(group, -(k + 1), 8) + core

    second = []
    for k in range(7):
        for j in range(2):
            part = blocks.at[sender(k), quarter(turn(x, j, 4))]
            at = 2 * k + j
            remote(part, part, a_send.at[at], a_recv.at[at], same[k]).wait_recv()
            copy = remote(part, part, b_send.at[at], b_recv.at[at], along_x(1 - 2 * j))
            copy.start()
            second.append(copy)

    for run in range(2):
        for part in range(ROWS // 128):
            pair = slice(128 * part, 128 * (part + 1))
            q_cols[run, :, pair] = q_rows[run, pair, :].T
    loads[2].wait()
    for part in range(LAT // 128):
        lanes = slice(128 * part, 128 * (part + 1))
        g_wide[part] = g_in[:, lanes].astype(F32)
        for h in range(HEADS):
            rows = g_wide[part, pl.ds(h, TOK, HEADS), :].astype(BF16)
            for run in range(2):
                g_rows[run, RUN * h : RUN * (h + 1), lanes] = rows[RUN * run : RUN * (run + 1)]
    for run in range(2):
        for part in range(ROWS // 128):
            pair = slice(128 * part, 128 * (part + 1))
            g_cols[run, :, pair] = g_rows[run, pair, :].T

    for copy in small:
        copy.wait()
    lane = lax.broadcasted_iota(I32, (N_CTX, TOK), 1)
    device = lax.broadcasted_iota(I32, (N_CTX, TOK), 0)
    at = jnp.concatenate([places[d] for d in range(N_CTX)], axis=0)
    holder = jnp.where(at[:, :1] // RUN == lane, 2 * device, 0)
    holder = holder + jnp.where(at[:, RUN : RUN + 1] // RUN == lane, 2 * device + 1, 0)
    info[:N_CTX] = at
    info[INVERSE : INVERSE + 1] = jnp.sum(holder, axis=0, keepdims=True)
    for value in range(1, N_DOCS):
        count = jnp.sum((docs[...] < value).astype(I32), keepdims=True)
        info[STARTS + value - 1 : STARTS + value] = jnp.broadcast_to(count, (1, TOK))
    copy = pltpu.make_async_copy(info, table, info_sem)
    copy.start()
    copy.wait()

    for k in range(7):
        block = blocks.at[sender(k)]
        for j in range(2):
            part = blocks.at[sender(k), quarter(turn(x, 3 - j, 4))]
            at = 2 * k + j
            remote(part, part, b_send.at[at], b_recv.at[at], along_x(1 - 2 * j)).wait_recv()
        copy = remote(block, block, c_send.at[k], c_recv.at[k], twin)
        copy.start()
        to_twin.append(copy)
    for copy in first + second + to_twin:
        copy.wait_send()
    for k in range(8):
        block = blocks.at[turn(sender(k), 1 - 2 * core, N_CTX)]
        remote(block, block, c_send.at[k], c_recv.at[k], twin).wait_recv()

    bounds = [table[STARTS + index, 0] for index in range(N_DOCS - 1)]
    low = lax.broadcasted_iota(I32, (WIDTH, TOK), 1) < RUN
    bases = [table[ctx, RUN * run] for run in range(2)]
    tops = [base // TOK - (SLOTS - 1) for base in bases]

    for run in range(2):
        for slot in range(SLOTS):
            tile = jnp.clip(tops[run] + slot, 0, N_CTX - 1)
            one, two = (jnp.clip(table[INVERSE, 2 * tile + i], 0, 2 * N_CTX - 1) for i in range(2))
            left, right = blocks[one // 2].astype(F32), blocks[two // 2].astype(F32)
            left = jnp.where(one % 2 == 0, left, pltpu.roll(left, RUN, 1))
            right = jnp.where(two % 2 == 1, right, pltpu.roll(right, RUN, 1))
            keys[run, :, TOK * slot : TOK * (slot + 1)] = jnp.where(low, left, right).astype(BF16)

        position = bases[run] + lax.broadcasted_iota(I32, (ROWS, 1), 0) % RUN
        begin = jnp.zeros((ROWS, 1), I32)
        for bound in bounds:
            begin = jnp.where(position >= bound, bound, begin)
        begin = begin - tops[run] * TOK
        position = position - tops[run] * TOK

        peak = jnp.full((ROWS, TOK), -1e30, F32)
        for start in range(0, SPAN, 2 * TOK):
            size = min(2 * TOK, SPAN - start)
            columns = slice(start, start + size)
            key = start + lax.broadcasted_iota(I32, (ROWS, size), 1)
            allowed = key >= begin
            if start + size == SPAN:
                allowed = allowed & (key <= position)
            value = jnp.where(allowed, dot(q_rows[run], keys[run, :, columns]), -1e30)
            score[:, columns] = value
            grad_p[:, columns] = dot(g_rows[run], keys[run, :LAT, columns])
            for part in range(size // TOK):
                peak = jnp.maximum(peak, value[:, TOK * part : TOK * (part + 1)])
        peak = jnp.max(peak, axis=1, keepdims=True) * (SCALE * LOG2E)

        sums = jnp.zeros((ROWS, TOK), F32)
        mixed = jnp.zeros((ROWS, TOK), F32)
        for slot in range(SLOTS):
            columns = slice(TOK * slot, TOK * (slot + 1))
            weight = jnp.exp2(score[:, columns] * (SCALE * LOG2E) - peak)
            score[:, columns] = weight
            sums = sums + weight
            mixed = mixed + weight * grad_p[:, columns]
        inverse = 1.0 / jnp.sum(sums, axis=1, keepdims=True)
        delta = jnp.sum(mixed, axis=1, keepdims=True) * inverse
        scaled = inverse * SCALE
        for slot in range(SLOTS):
            columns = slice(TOK * slot, TOK * (slot + 1))
            weight = score[:, columns]
            prob[run, :, columns] = (weight * inverse).astype(BF16)
            grad_s[run, :, columns] = (weight * scaled * (grad_p[:, columns] - delta)).astype(BF16)

    def gradient(rows, target):
        size = rows.stop - rows.start
        values = slice(rows.start, min(rows.stop, LAT))
        for run in range(2):
            for start in range(0, SPAN, 2 * TOK):
                width = min(2 * TOK, SPAN - start)
                columns = slice(start, start + width)
                both = dot(q_cols[run, rows, :], grad_s[run, :, columns])
                value = dot(g_cols[run, values, :], prob[run, :, columns])
                if values.stop < rows.stop:
                    value = jnp.concatenate(
                        [value, jnp.zeros((rows.stop - values.stop, width), F32)], axis=0
                    )
                both = both + value
                for part in range(width // TOK):
                    dkv[run, start // TOK + part, :size] = both[:, TOK * part : TOK * (part + 1)]
        first_lanes = lax.broadcasted_iota(I32, (size, TOK), 1) < RUN
        for device in range(N_CTX):
            out = []
            for half in range(2):
                place = table[device, RUN * half] // RUN
                found = jnp.zeros((size, TOK), F32)
                for run in range(2):
                    slot = place // 2 - tops[run]
                    inside = (slot >= 0) & (slot < SLOTS)
                    term = dkv[run, jnp.clip(slot, 0, SLOTS - 1), :size]
                    found = found + jnp.where(inside, term, 0.0)
                out.append(jnp.where(place % 2 == half, found, pltpu.roll(found, RUN, 1)))
            target[device % 2, device // 2] = jnp.where(first_lanes, out[0], out[1]).astype(BF16)

    def query_gradient(run):
        dq[run] = dot_nt(grad_s[run], keys[run])

    gradient(slice(0, X_ROWS), x_part)
    x_swap = remote(x_part.at[1 - core], x_twin, t_send.at[0], t_recv.at[0], twin)
    x_swap.start()
    gradient(slice(X_ROWS, WIDTH), y_part)
    y_swap = remote(y_part.at[1 - core], y_twin, t_send.at[1], t_recv.at[1], twin)
    y_swap.start()

    def x_rows(index):
        return pl.ds(pl.multiple_of(X_PIECE * index, 16), X_PIECE)

    def y_rows(index):
        return pl.ds(pl.multiple_of(Y_PIECE * index, 16), Y_PIECE)

    x_swap.wait_recv()
    for g in range(8):
        x_chip[g] = (x_part[core, g].astype(F32) + x_twin[g].astype(F32)).astype(BF16)
    x_step = []
    for k in range(3):
        source = x_chip.at[:, x_rows(turn(x, k + 1, 4))]
        copy = remote(source, x_recv.at[k], x_send.at[k], x_got.at[k], along_x(k + 1))
        copy.start()
        x_step.append(copy)
    y_swap.wait_recv()
    for g in range(8):
        y_chip[g] = (y_part[core, g].astype(F32) + y_twin[g].astype(F32)).astype(BF16)
    y_step = []
    for k in range(7):
        source = y_chip.at[turn(group, k + 1, 8)]
        copy = remote(source, y_recv.at[k], y_send.at[k], y_got.at[k], same[k])
        copy.start()
        y_step.append(copy)

    for run in range(2):
        query_gradient(run)
    for h in range(HEADS):
        rows = slice(RUN * h, RUN * (h + 1))
        both = jnp.concatenate([dq[0, rows, :], dq[1, rows, :]], axis=0)
        d_query[h] = both.T.astype(BF16)

    for copy in x_step:
        copy.wait_recv()
    for g in range(8):
        total = x_chip[g, x_rows(x), :].astype(F32)
        for k in range(3):
            total = total + x_recv[k, g].astype(F32)
        x_sum[g] = total.astype(BF16)
    x_end = []
    for k, device in enumerate(plane):
        copy = remote(
            x_sum.at[turn(group, (k + 1) % 8, 8)], x_last.at[k], xl_send.at[k], xl_got.at[k], device
        )
        copy.start()
        x_end.append(copy)
    for copy in y_step:
        copy.wait_recv()
    total = y_chip[group].astype(F32)
    for k in range(7):
        total = total + y_recv[k].astype(F32)
    y_sum[...] = total.astype(BF16)
    y_end = []
    for k, device in enumerate(over_tp):
        source = y_sum.at[y_rows(turn(tp, k + 1, N_TP) // 2)]
        copy = remote(source, y_last.at[k], yl_send.at[k], yl_got.at[k], device)
        copy.start()
        y_end.append(copy)

    for copy in x_end:
        copy.wait_recv()
    total = x_sum[group].astype(F32)
    for k in range(15):
        total = total + x_last[k].astype(F32)
    piece[:X_PIECE] = total.astype(BF16)
    for copy in y_end:
        copy.wait_recv()
    total = y_sum[y_rows(x), :].astype(F32)
    for k in range(7):
        total = total + y_last[k].astype(F32)
    piece[X_PIECE:] = total.astype(BF16)
    out_step = []
    for k in range(3):
        copy = remote(piece, pieces.at[k], o_send.at[k], o_recv.at[k], along_x(k + 1))
        copy.start()
        out_step.append(copy)

    def place(index, value):
        d_latent[x_rows(index), :] = value[:X_PIECE]
        d_latent[pl.ds(pl.multiple_of(X_ROWS + Y_PIECE * index, 16), Y_PIECE), :] = value[X_PIECE:]

    place(x, piece[...])
    for k in range(3):
        out_step[k].wait_recv()
        place(turn(x, -(k + 1), 4), pieces[k])
    for copy in [x_swap, y_swap] + x_step + y_step + x_end + y_end + out_step:
        copy.wait_send()


def local(query, latent, d_out, positions, doc_ids):
    whole, fast = pl.BlockSpec(memory_space=pl.ANY), pl.BlockSpec(memory_space=pltpu.VMEM)
    vmem, dma = pltpu.VMEM, pltpu.SemaphoreType.DMA
    d_query, d_latent = pl.pallas_call(
        kernel,
        out_shape=[
            jax.ShapeDtypeStruct((HEADS, WIDTH, TOK), BF16),
            jax.ShapeDtypeStruct((WIDTH, TOK), BF16),
        ],
        in_specs=[whole, fast, fast, whole, whole],
        out_specs=[fast, fast],
        scratch_shapes=[
            vmem((HEADS, WIDTH, TOK), BF16),
            vmem((TOK * HEADS, LAT), BF16),
            vmem((LAT // 128, TOK * HEADS, 128), F32),
            vmem((2, ROWS, WIDTH), BF16),
            vmem((2, WIDTH, ROWS), BF16),
            vmem((2, ROWS, LAT), BF16),
            vmem((2, LAT, ROWS), BF16),
            vmem((N_CTX, WIDTH, TOK), BF16),
            vmem((N_CTX, 1, TOK), I32),
            vmem((24, TOK), I32),
            pltpu.SMEM((24, TOK), I32),
            vmem((2, WIDTH, SPAN), BF16),
            vmem((ROWS, SPAN), F32),
            vmem((ROWS, SPAN), F32),
            vmem((2, ROWS, SPAN), BF16),
            vmem((2, ROWS, SPAN), BF16),
            vmem((2, SLOTS, X_ROWS, TOK), F32),
            vmem((2, ROWS, WIDTH), F32),
            vmem((2, 8, X_ROWS, TOK), BF16),
            vmem((2, 8, Y_ROWS, TOK), BF16),
            vmem((8, X_ROWS, TOK), BF16),
            vmem((8, Y_ROWS, TOK), BF16),
            vmem((8, X_ROWS, TOK), BF16),
            vmem((8, Y_ROWS, TOK), BF16),
            vmem((3, 8, X_PIECE, TOK), BF16),
            vmem((7, Y_ROWS, TOK), BF16),
            vmem((8, X_PIECE, TOK), BF16),
            vmem((Y_ROWS, TOK), BF16),
            vmem((15, X_PIECE, TOK), BF16),
            vmem((7, Y_PIECE, TOK), BF16),
            vmem((X_PIECE + Y_PIECE, TOK), BF16),
            vmem((3, X_PIECE + Y_PIECE, TOK), BF16),
            dma((3,)),
            dma,
        ]
        + [dma((size,)) for size in (14, 14, 8, 15, 2, 3, 7, 15, 7, 3) for _ in range(2)],
        compiler_params=pltpu.CompilerParams(
            collective_id=0, has_side_effects=True, vmem_limit_bytes=63 << 20
        ),
        name="latent_attention_backward",
    )(
        latent.T,
        positions.reshape(1, TOK),
        doc_ids.reshape(-1, TOK),
        query.transpose(1, 2, 0),
        d_out.reshape(TOK * HEADS, LAT),
    )
    return (d_query.transpose(2, 0, 1), d_latent.T)


def solution(mesh):
    return jax.shard_map(
        local,
        mesh=mesh,
        in_specs=(P("ctx", "tp", None), P("ctx", None), P("ctx", "tp", None), P("ctx"), P()),
        out_specs=(P("ctx", "tp", None), P("ctx", None)),
        check_vma=False,
    )
```

```python
import jax
import jax.numpy as jnp
from jax import lax
from jax.experimental import pallas as pl
from jax.experimental.pallas import tpu as pltpu
from jax.sharding import PartitionSpec as P

MESH = pl.DeviceIdType.MESH
F32, BF16, I32 = jnp.float32, jnp.bfloat16, jnp.int32
SCALE = 192.0 ** (-0.5)
LOG2E = 1.4426950408889634
WIDTH, LAT, TOK, HEADS, RUN = 576, 512, 128, 8, 64
ROWS = HEADS * RUN
N_CTX, N_TP, N_DOCS = 16, 8, 4
SLOTS = 9
SPAN = SLOTS * TOK
QUARTER = WIDTH // 4
X_SIZES, Y_SIZE = (48, 32), 32
X_PIECE, PIECE = 80, 144
BASES = (0, 192, 320, 448, 576)
INVERSE, STARTS = N_CTX, N_CTX + 1


def dot(left, right):
    return jnp.dot(left, right, preferred_element_type=F32)


def dot_nt(left, right):
    return lax.dot_general(left, right, (((1,), (1,)), ((), ())), preferred_element_type=F32)


def remote(src, dst, send, recv, device):
    return pltpu.make_async_remote_copy(
        src_ref=src, dst_ref=dst, send_sem=send, recv_sem=recv, device_id=device, device_id_type=MESH
    )


def kernel(
    latent, positions, docs, query, d_out, d_query, d_latent,
    q_in, g_in, g_wide, q_rows, q_cols, g_rows, g_cols, blocks, places, info, table,
    keys, score, grad_p, prob, grad_s, dkv, dq,
    x_part0, y_part0, x_part1, y_part1, x_twin0, y_twin0, x_twin1, y_twin1,
    x_recv0, y_recv0, x_recv1, y_recv1, x_sum, y_sum,
    x_last, y_last, piece, pieces, raw, total_rows, docs_in,
    in_sem, info_sem, a_send, a_recv, b_send, b_recv, c_send, c_recv, pos_send, pos_recv,
    t_send, t_recv, x_send, x_got, y_send, y_got, xl_send, xl_got, yl_send, yl_got, o_send, o_recv,
):
    ctx, tp = lax.axis_index("ctx"), lax.axis_index("tp")
    core, group = lax.rem(ctx, 2), ctx // 2
    x, low_z = tp // 2, lax.rem(tp, 2)

    def turn(index, step, size):
        return lax.rem(index + step + size, size)

    def along_x(step):
        return (ctx, 2 * turn(x, step, 4) + low_z)

    y, high_z = group // 2, lax.rem(group, 2)
    me = 8 * core + group
    twin = (2 * group + 1 - core, tp)
    mates, targets, sources = [], [], []
    for k in range(1, 8):
        flip, step = k // 4, k % 4
        over = 1 - high_z if flip else high_z
        targets.append(2 * turn(y, step, 4) + over)
        sources.append(2 * turn(y, -step, 4) + over)
        mates.append((2 * targets[-1] + core, 2 * x + (1 - low_z if flip else low_z)))
    over_tp = [(ctx, turn(tp, k, N_TP)) for k in range(1, N_TP)]
    plane = [
        (2 * turn(group, k, 8) + core, 2 * x + turn(low_z, j, 2))
        for j in range(2) for k in range(8) if j or k
    ]

    friends = mates + [twin, along_x(1), along_x(-1), plane[7]]
    barrier = pltpu.get_barrier_semaphore()
    for device in friends:
        pl.semaphore_signal(barrier, inc=1, device_id=device, device_id_type=MESH)
    loads = [
        pltpu.make_async_copy(positions, places.at[core, group], in_sem.at[3]),
        pltpu.make_async_copy(latent, raw, in_sem.at[0]),
        pltpu.make_async_copy(query, q_in, in_sem.at[1]),
        pltpu.make_async_copy(d_out, g_in, in_sem.at[2]),
        pltpu.make_async_copy(docs, docs_in, in_sem.at[4]),
    ]
    for copy in loads:
        copy.start()
    loads[0].wait()
    swapped = jnp.broadcast_to(places[core, group][:, :1] // RUN % 2 == 1, (WIDTH, TOK))

    def even_first(value):
        value = value.astype(F32)
        return jnp.where(swapped, pltpu.roll(value, RUN, 1), value).astype(BF16)

    loads[1].wait()
    blocks[me] = even_first(raw[...])
    pl.semaphore_wait(barrier, len(friends))

    def quarter(index):
        return pl.ds(pl.multiple_of(QUARTER * index, 16), QUARTER)

    first, small = [], []
    for j in range(2):
        for k, device in enumerate(mates):
            part = blocks.at[me, quarter(turn(x, j, 4))]
            copy = remote(part, part, a_send.at[2 * k + j], a_recv.at[2 * k + j], device)
            copy.start()
            first.append(copy)
    for k, device in enumerate(mates):
        here = places.at[core, group]
        copy = remote(here, here, pos_send.at[k], pos_recv.at[k], device)
        copy.start()
        small.append(copy)
    to_twin = [remote(blocks.at[me], blocks.at[me], c_send.at[7], c_recv.at[7], twin)]
    to_twin[0].start()

    loads[2].wait()
    for h in range(HEADS):
        rows = q_in[h].T
        for run in range(2):
            q_rows[run, RUN * h : RUN * (h + 1), :] = rows[RUN * run : RUN * (run + 1)]

    second = []
    for j in range(2):
        for k in range(7):
            part = blocks.at[8 * core + sources[k], quarter(turn(x, j, 4))]
            at = 2 * k + j
            remote(part, part, a_send.at[at], a_recv.at[at], mates[k]).wait_recv()
            copy = remote(part, part, b_send.at[at], b_recv.at[at], along_x(1 - 2 * j))
            copy.start()
            second.append(copy)
    for k in range(7):
        here = places.at[core, sources[k]]
        remote(here, here, pos_send.at[k], pos_recv.at[k], mates[k]).wait_recv()
    here = places.at[core]
    copy = remote(here, here, pos_send.at[7], pos_recv.at[7], twin)
    copy.start()
    small.append(copy)

    for run in range(2):
        for part in range(ROWS // 128):
            pair = slice(128 * part, 128 * (part + 1))
            q_cols[run, :, pair] = q_rows[run, pair, :].T
    loads[3].wait()
    for part in range(LAT // 128):
        lanes = slice(128 * part, 128 * (part + 1))
        g_wide[part] = g_in[:, lanes].astype(F32)
        for h in range(HEADS):
            rows = g_wide[part, pl.ds(h, TOK, HEADS), :].astype(BF16)
            for run in range(2):
                g_rows[run, RUN * h : RUN * (h + 1), lanes] = rows[RUN * run : RUN * (run + 1)]
    for run in range(2):
        for part in range(ROWS // 128):
            pair = slice(128 * part, 128 * (part + 1))
            g_cols[run, :, pair] = g_rows[run, pair, :].T

    here = places.at[1 - core]
    remote(here, here, pos_send.at[7], pos_recv.at[7], twin).wait_recv()
    lane = lax.broadcasted_iota(I32, (N_CTX, TOK), 1)
    row = lax.broadcasted_iota(I32, (N_CTX, TOK), 0)
    at = jnp.concatenate([places[d // 8, d % 8] for d in range(N_CTX)], axis=0)
    one, two = at[:, :1] // RUN, at[:, RUN : RUN + 1] // RUN
    holder = jnp.where((one == lane) | (two == lane), row, 0)
    info[:N_CTX] = at
    info[INVERSE : INVERSE + 1] = jnp.sum(holder, axis=0, keepdims=True)
    loads[4].wait()
    for value in range(1, N_DOCS):
        count = jnp.sum((docs_in[...] < value).astype(I32), keepdims=True)
        info[STARTS + value - 1 : STARTS + value] = jnp.broadcast_to(count, (1, TOK))
    copy = pltpu.make_async_copy(info, table, info_sem)
    copy.start()
    copy.wait()

    for k in range(7):
        block = blocks.at[8 * core + sources[k]]
        for j in range(2):
            part = blocks.at[8 * core + sources[k], quarter(turn(x, 3 - j, 4))]
            at = 2 * k + j
            remote(part, part, b_send.at[at], b_recv.at[at], along_x(1 - 2 * j)).wait_recv()
        copy = remote(block, block, c_send.at[k], c_recv.at[k], twin)
        copy.start()
        to_twin.append(copy)
    for copy in first + second + to_twin + small:
        copy.wait_send()
    for k in range(8):
        block = blocks.at[8 * (1 - core) + (sources + [group])[k]]
        remote(block, block, c_send.at[k], c_recv.at[k], twin).wait_recv()

    bounds = [table[STARTS + index, 0] for index in range(N_DOCS - 1)]
    low = lax.broadcasted_iota(I32, (WIDTH, TOK), 1) < RUN
    bases = [table[me, RUN * run] for run in range(2)]
    tops = [base // TOK - (SLOTS - 1) for base in bases]

    for run in range(2):
        for slot in range(SLOTS):
            tile = jnp.clip(tops[run] + slot, 0, N_CTX - 1)
            one, two = (jnp.clip(table[INVERSE, 2 * tile + i], 0, N_CTX - 1) for i in range(2))
            keys[run, :, TOK * slot : TOK * (slot + 1)] = jnp.where(low, blocks[one], blocks[two])

        position = bases[run] + lax.broadcasted_iota(I32, (ROWS, 1), 0) % RUN
        begin = jnp.zeros((ROWS, 1), I32)
        for bound in bounds:
            begin = jnp.where(position >= bound, bound, begin)
        begin = begin - tops[run] * TOK
        position = position - tops[run] * TOK

        peak = jnp.full((ROWS, TOK), -1e30, F32)
        for start in range(0, SPAN, 2 * TOK):
            size = min(2 * TOK, SPAN - start)
            columns = slice(start, start + size)
            key = start + lax.broadcasted_iota(I32, (ROWS, size), 1)
            allowed = key >= begin
            if start + size == SPAN:
                allowed = allowed & (key <= position)
            value = jnp.where(allowed, dot(q_rows[run], keys[run, :, columns]), -1e30)
            score[:, columns] = value
            grad_p[:, columns] = dot(g_rows[run], keys[run, :LAT, columns])
            for part in range(size // TOK):
                peak = jnp.maximum(peak, value[:, TOK * part : TOK * (part + 1)])
        peak = jnp.max(peak, axis=1, keepdims=True) * (SCALE * LOG2E)

        sums = jnp.zeros((ROWS, TOK), F32)
        mixed = jnp.zeros((ROWS, TOK), F32)
        for slot in range(SLOTS):
            columns = slice(TOK * slot, TOK * (slot + 1))
            weight = jnp.exp2(score[:, columns] * (SCALE * LOG2E) - peak)
            score[:, columns] = weight
            sums = sums + weight
            mixed = mixed + weight * grad_p[:, columns]
        inverse = 1.0 / jnp.sum(sums, axis=1, keepdims=True)
        delta = jnp.sum(mixed, axis=1, keepdims=True) * inverse
        scaled = inverse * SCALE
        for slot in range(SLOTS):
            columns = slice(TOK * slot, TOK * (slot + 1))
            weight = score[:, columns]
            prob[run, :, columns] = (weight * inverse).astype(BF16)
            grad_s[run, :, columns] = (weight * scaled * (grad_p[:, columns] - delta)).astype(BF16)

    def gradient(rows, target):
        size = rows.stop - rows.start
        values = slice(rows.start, min(rows.stop, LAT))
        for run in range(2):
            for start in range(0, SPAN, 2 * TOK):
                width = min(2 * TOK, SPAN - start)
                columns = slice(start, start + width)
                both = dot(q_cols[run, rows, :], grad_s[run, :, columns])
                value = dot(g_cols[run, values, :], prob[run, :, columns])
                if values.stop < rows.stop:
                    value = jnp.concatenate(
                        [value, jnp.zeros((rows.stop - values.stop, width), F32)], axis=0
                    )
                both = both + value
                for part in range(width // TOK):
                    dkv[run, start // TOK + part, :size] = both[:, TOK * part : TOK * (part + 1)]
        first_lanes = lax.broadcasted_iota(I32, (size, TOK), 1) < RUN
        for device in range(N_CTX):
            out = []
            runs = [table[device, RUN * half] // RUN for half in range(2)]
            for parity in range(2):
                tile = jnp.where(runs[0] % 2 == parity, runs[0], runs[1]) // 2
                found = jnp.zeros((size, TOK), F32)
                for run in range(2):
                    slot = tile - tops[run]
                    inside = (slot >= 0) & (slot < SLOTS)
                    term = dkv[run, jnp.clip(slot, 0, SLOTS - 1), :size]
                    found = found + jnp.where(inside, term, 0.0)
                out.append(found)
            target[device // 8, device % 8] = jnp.where(first_lanes, out[0], out[1]).astype(BF16)

    def query_gradient(run):
        dq[run] = dot_nt(grad_s[run], keys[run])

    def rows_of(index, size):
        return pl.ds(pl.multiple_of(size * index, 16), size)

    swaps, x_step, y_step = [], [], []
    chip = [x_part0, y_part0, x_part1, y_part1]
    twin_part = [x_twin0, y_twin0, x_twin1, y_twin1]
    x_recv = [x_recv0, x_recv1]
    y_recv = [y_recv0, y_recv1]

    def to_twin_core(c):
        copy = remote(chip[c].at[1 - core], twin_part[c], t_send.at[c], t_recv.at[c], twin)
        copy.start()
        swaps.append(copy)

    def over_links(c):
        swaps[c].wait_recv()
        ours = chip[c]
        for g in range(8):
            ours[core, g] = (ours[core, g].astype(F32) + twin_part[c][g].astype(F32)).astype(BF16)
        half = c // 2
        if c % 2 == 0:
            size = X_SIZES[half]
            for k in range(3):
                source = ours.at[core, :, rows_of(turn(x, k + 1, 4), size)]
                at = 3 * half + k
                copy = remote(source, x_recv[half].at[k], x_send.at[at], x_got.at[at], along_x(k + 1))
                copy.start()
                x_step.append(copy)
        else:
            for k in range(7):
                source = ours.at[core, targets[k]]
                at = 7 * half + k
                copy = remote(source, y_recv[half].at[k], y_send.at[at], y_got.at[at], mates[k])
                copy.start()
                y_step.append(copy)

    for c in range(4):
        gradient(slice(BASES[c], BASES[c + 1]), chip[c])
        to_twin_core(c)
        if c:
            over_links(c - 1)
    over_links(3)

    for run in range(2):
        query_gradient(run)
    for h in range(HEADS):
        rows = slice(RUN * h, RUN * (h + 1))
        both = jnp.concatenate([dq[0, rows, :], dq[1, rows, :]], axis=0)
        q_in[h] = both.T.astype(BF16)
    store = pltpu.make_async_copy(q_in, d_query, in_sem.at[2])
    store.start()

    for copy in x_step:
        copy.wait_recv()
    for half in range(2):
        size, first_row = X_SIZES[half], half * X_SIZES[0]
        for g in range(8):
            total = chip[2 * half][core, g, rows_of(x, size), :].astype(F32)
            for k in range(3):
                total = total + x_recv[half][k, g].astype(F32)
            x_sum[g, first_row : first_row + size] = total.astype(BF16)
    x_end = []
    for k, device in enumerate(plane):
        copy = remote(
            x_sum.at[turn(group, (k + 1) % 8, 8)], x_last.at[k], xl_send.at[k], xl_got.at[k], device
        )
        copy.start()
        x_end.append(copy)
    for copy in y_step:
        copy.wait_recv()
    for half in range(2):
        total = chip[2 * half + 1][core, group].astype(F32)
        for k in range(7):
            total = total + y_recv[half][k].astype(F32)
        y_sum[half] = total.astype(BF16)
    y_end = []
    for k, device in enumerate(over_tp):
        source = y_sum.at[:, rows_of(turn(tp, k + 1, N_TP) // 2, Y_SIZE)]
        copy = remote(source, y_last.at[k], yl_send.at[k], yl_got.at[k], device)
        copy.start()
        y_end.append(copy)

    for copy in x_end:
        copy.wait_recv()
    total = x_sum[group].astype(F32)
    for k in range(15):
        total = total + x_last[k].astype(F32)
    piece[:X_PIECE] = total.astype(BF16)
    for copy in y_end:
        copy.wait_recv()
    for half in range(2):
        total = y_sum[half, rows_of(x, Y_SIZE), :].astype(F32)
        for k in range(7):
            total = total + y_last[k, half].astype(F32)
        piece[X_PIECE + half * Y_SIZE : X_PIECE + (half + 1) * Y_SIZE] = total.astype(BF16)
    out_step = []
    for k in range(3):
        copy = remote(piece, pieces.at[k], o_send.at[k], o_recv.at[k], along_x(k + 1))
        copy.start()
        out_step.append(copy)

    def place(index, value):
        first_row = 0
        for c in (0, 2, 1, 3):
            size = X_SIZES[c // 2] if c % 2 == 0 else Y_SIZE
            at = pl.ds(pl.multiple_of(BASES[c] + size * index, 16), size)
            total_rows[at, :] = value[first_row : first_row + size]
            first_row += size

    place(x, piece[...])
    for k in range(3):
        out_step[k].wait_recv()
        place(turn(x, -(k + 1), 4), pieces[k])
    d_latent[...] = even_first(total_rows[...])
    store.wait()
    for copy in swaps + x_step + y_step + x_end + y_end + out_step:
        copy.wait_send()


def local(query, latent, d_out, positions, doc_ids):
    whole, fast = pl.BlockSpec(memory_space=pl.ANY), pl.BlockSpec(memory_space=pltpu.VMEM)
    vmem, dma = pltpu.VMEM, pltpu.SemaphoreType.DMA
    d_query, d_latent = pl.pallas_call(
        kernel,
        out_shape=[
            jax.ShapeDtypeStruct((HEADS, WIDTH, TOK), BF16),
            jax.ShapeDtypeStruct((WIDTH, TOK), BF16),
        ],
        in_specs=[whole] * 5,
        out_specs=[whole, fast],
        scratch_shapes=[
            vmem((HEADS, WIDTH, TOK), BF16),
            vmem((TOK * HEADS, LAT), BF16),
            vmem((LAT // 128, TOK * HEADS, 128), F32),
            vmem((2, ROWS, WIDTH), BF16),
            vmem((2, WIDTH, ROWS), BF16),
            vmem((2, ROWS, LAT), BF16),
            vmem((2, LAT, ROWS), BF16),
            vmem((N_CTX, WIDTH, TOK), BF16),
            vmem((2, 8, 1, TOK), I32),
            vmem((24, TOK), I32),
            pltpu.SMEM((24, TOK), I32),
            vmem((2, WIDTH, SPAN), BF16),
            vmem((ROWS, SPAN), F32),
            vmem((ROWS, SPAN), F32),
            vmem((2, ROWS, SPAN), BF16),
            vmem((2, ROWS, SPAN), BF16),
            vmem((2, SLOTS, BASES[1], TOK), F32),
            vmem((2, ROWS, WIDTH), F32),
        ]
        + [vmem((2, 8, BASES[c + 1] - BASES[c], TOK), BF16) for c in range(4)]
        + [vmem((8, BASES[c + 1] - BASES[c], TOK), BF16) for c in range(4)]
        + [
            vmem((3, 8, X_SIZES[0], TOK), BF16),
            vmem((7, 4 * Y_SIZE, TOK), BF16),
            vmem((3, 8, X_SIZES[1], TOK), BF16),
            vmem((7, 4 * Y_SIZE, TOK), BF16),
            vmem((8, X_PIECE, TOK), BF16),
            vmem((2, 4 * Y_SIZE, TOK), BF16),
            vmem((15, X_PIECE, TOK), BF16),
            vmem((7, 2, Y_SIZE, TOK), BF16),
            vmem((PIECE, TOK), BF16),
            vmem((3, PIECE, TOK), BF16),
            vmem((WIDTH, TOK), BF16),
            vmem((WIDTH, TOK), BF16),
            vmem((N_CTX, TOK), I32),
            dma((5,)),
            dma,
        ]
        + [dma((size,)) for size in (14, 14, 8, 8, 4, 6, 14, 15, 7, 3) for _ in range(2)],
        compiler_params=pltpu.CompilerParams(
            collective_id=0, has_side_effects=True, vmem_limit_bytes=63 << 20
        ),
        name="latent_attention_backward",
    )(
        latent.T,
        positions.reshape(1, TOK),
        doc_ids.reshape(-1, TOK),
        query.transpose(1, 2, 0),
        d_out.reshape(TOK * HEADS, LAT),
    )
    return (d_query.transpose(2, 0, 1), d_latent.T)


def solution(mesh):
    return jax.shard_map(
        local,
        mesh=mesh,
        in_specs=(P("ctx", "tp", None), P("ctx", None), P("ctx", "tp", None), P("ctx"), P()),
        out_specs=(P("ctx", "tp", None), P("ctx", None)),
        check_vma=False,
    )
```

```python
import jax
import jax.numpy as jnp
from jax import lax
from jax.experimental import pallas as pl
from jax.experimental.pallas import tpu as pltpu
from jax.sharding import PartitionSpec as P

MESH = pl.DeviceIdType.MESH
F32, BF16, I32 = jnp.float32, jnp.bfloat16, jnp.int32
SCALE = 192.0 ** (-0.5)
LOG2E = 1.4426950408889634
WIDTH, LAT, TOK, HEADS, RUN = 576, 512, 128, 8, 64
ROWS = HEADS * RUN
N_CTX, N_TP, N_DOCS = 16, 8, 4
SLOTS = 9
SPAN = SLOTS * TOK
QUARTER = WIDTH // 4
X_SIZES, Y_SIZE = (32, 48), 32
X_BOTH, X_PIECE, PIECE = 80, 48, 80
BASES = (0, 128, 256, 448, 576)
CHUNK = 192
INVERSE, STARTS = N_CTX, N_CTX + 1


def dot(left, right):
    return jnp.dot(left, right, preferred_element_type=F32)


def dot_nt(left, right):
    return lax.dot_general(left, right, (((1,), (1,)), ((), ())), preferred_element_type=F32)


def remote(src, dst, send, recv, device):
    return pltpu.make_async_remote_copy(
        src_ref=src, dst_ref=dst, send_sem=send, recv_sem=recv, device_id=device, device_id_type=MESH
    )


def kernel(
    latent, positions, docs, query, d_out, d_query, pieces,
    q_in, g_in, g_wide, q_rows, q_cols, g_rows, g_cols, blocks, places, info, table,
    keys, score, grad_p, prob, grad_s, dkv, dq,
    x_part0, y_part0, x_part1, y_part1, x_twin0, y_twin0, x_twin1, y_twin1,
    x_recv0, y_recv0, x_recv1, y_recv1, x_sum, y_sum,
    x_last, y_last, piece, raw, docs_in,
    in_sem, info_sem, a_send, a_recv, b_send, b_recv, c_send, c_recv, pos_send, pos_recv,
    t_send, t_recv, x_send, x_got, y_send, y_got, xl_send, xl_got, yl_send, yl_got, o_send, o_recv,
):
    ctx, tp = lax.axis_index("ctx"), lax.axis_index("tp")
    core, group = lax.rem(ctx, 2), ctx // 2
    x, low_z = tp // 2, lax.rem(tp, 2)

    def turn(index, step, size):
        return lax.rem(index + step + size, size)

    def along_x(step):
        return (ctx, 2 * turn(x, step, 4) + low_z)

    y, high_z = group // 2, lax.rem(group, 2)
    me = 8 * core + group
    twin = (2 * group + 1 - core, tp)
    mates, targets, sources = [], [], []
    for k in range(1, 8):
        flip, step = k // 4, k % 4
        over = 1 - high_z if flip else high_z
        targets.append(2 * turn(y, step, 4) + over)
        sources.append(2 * turn(y, -step, 4) + over)
        mates.append((2 * targets[-1] + core, 2 * x + (1 - low_z if flip else low_z)))
    over_tp = [(ctx, turn(tp, k, N_TP)) for k in range(1, N_TP)]
    plane = [
        (2 * turn(group, k, 8) + core, 2 * x + turn(low_z, j, 2))
        for j in range(2) for k in range(8) if j or k
    ]

    friends = mates + [twin, along_x(1), along_x(-1), plane[7]]
    barrier = pltpu.get_barrier_semaphore()
    for device in friends:
        pl.semaphore_signal(barrier, inc=1, device_id=device, device_id_type=MESH)
    loads = [
        pltpu.make_async_copy(positions, places.at[core, group], in_sem.at[3]),
        pltpu.make_async_copy(latent, raw, in_sem.at[0]),
        pltpu.make_async_copy(query, q_in, in_sem.at[1]),
        pltpu.make_async_copy(d_out, g_in, in_sem.at[2]),
        pltpu.make_async_copy(docs, docs_in, in_sem.at[4]),
    ]
    for copy in loads:
        copy.start()
    loads[0].wait()
    loads[1].wait()
    blocks[me] = even_first(raw[...], places[core, group])
    pl.semaphore_wait(barrier, len(friends))

    def quarter(index):
        return pl.ds(pl.multiple_of(QUARTER * index, 16), QUARTER)

    first, small = [], []
    for turn_of in range(2):
        for k, device in enumerate(mates):
            j = (turn_of + k) % 2
            part = blocks.at[me, quarter(turn(x, j, 4))]
            copy = remote(part, part, a_send.at[2 * k + j], a_recv.at[2 * k + j], device)
            copy.start()
            first.append(copy)
    for k, device in enumerate(mates):
        here = places.at[core, group]
        copy = remote(here, here, pos_send.at[k], pos_recv.at[k], device)
        copy.start()
        small.append(copy)
    to_twin = [remote(blocks.at[me], blocks.at[me], c_send.at[28], c_recv.at[28], twin)]
    to_twin[0].start()

    loads[2].wait()
    for h in range(HEADS):
        rows = q_in[h].T
        for run in range(2):
            q_rows[run, RUN * h : RUN * (h + 1), :] = rows[RUN * run : RUN * (run + 1)]

    def share(k, i, block, index):
        part = block.at[quarter(index)]
        copy = remote(part, part, c_send.at[4 * k + i], c_recv.at[4 * k + i], twin)
        copy.start()
        to_twin.append(copy)

    second = []
    for turn_of in range(2):
        for k in range(7):
            j = (turn_of + k) % 2
            block = blocks.at[8 * core + sources[k]]
            part = block.at[quarter(turn(x, j, 4))]
            at = 2 * k + j
            remote(part, part, a_send.at[at], a_recv.at[at], mates[k]).wait_recv()
            copy = remote(part, part, b_send.at[at], b_recv.at[at], along_x(1 - 2 * j))
            copy.start()
            second.append(copy)
            share(k, j, block, turn(x, j, 4))
    for k in range(7):
        here = places.at[core, sources[k]]
        remote(here, here, pos_send.at[k], pos_recv.at[k], mates[k]).wait_recv()
    here = places.at[core]
    copy = remote(here, here, pos_send.at[7], pos_recv.at[7], twin)
    copy.start()
    small.append(copy)

    for run in range(2):
        for part in range(ROWS // 128):
            pair = slice(128 * part, 128 * (part + 1))
            q_cols[run, :, pair] = q_rows[run, pair, :].T
    loads[3].wait()
    for part in range(LAT // 128):
        lanes = slice(128 * part, 128 * (part + 1))
        g_wide[part] = g_in[:, lanes].astype(F32)
        for h in range(HEADS):
            rows = g_wide[part, pl.ds(h, TOK, HEADS), :].astype(BF16)
            for run in range(2):
                g_rows[run, RUN * h : RUN * (h + 1), lanes] = rows[RUN * run : RUN * (run + 1)]
    for run in range(2):
        for part in range(ROWS // 128):
            pair = slice(128 * part, 128 * (part + 1))
            g_cols[run, :, pair] = g_rows[run, pair, :].T

    here = places.at[1 - core]
    remote(here, here, pos_send.at[7], pos_recv.at[7], twin).wait_recv()
    lane = lax.broadcasted_iota(I32, (N_CTX, TOK), 1)
    row = lax.broadcasted_iota(I32, (N_CTX, TOK), 0)
    at = jnp.concatenate([places[d // 8, d % 8] for d in range(N_CTX)], axis=0)
    one, two = at[:, :1] // RUN, at[:, RUN : RUN + 1] // RUN
    holder = jnp.where((one == lane) | (two == lane), row, 0)
    info[:N_CTX] = at
    info[INVERSE : INVERSE + 1] = jnp.sum(holder, axis=0, keepdims=True)
    loads[4].wait()
    for value in range(1, N_DOCS):
        count = jnp.sum((docs_in[...] < value).astype(I32), keepdims=True)
        info[STARTS + value - 1 : STARTS + value] = jnp.broadcast_to(count, (1, TOK))
    copy = pltpu.make_async_copy(info, table, info_sem)
    copy.start()
    copy.wait()

    for turn_of in range(2):
        for k in range(7):
            j = (turn_of + k) % 2
            block = blocks.at[8 * core + sources[k]]
            part = block.at[quarter(turn(x, 3 - j, 4))]
            at = 2 * k + j
            remote(part, part, b_send.at[at], b_recv.at[at], along_x(1 - 2 * j)).wait_recv()
            share(k, 3 - j, block, turn(x, 3 - j, 4))
    for copy in first + second + to_twin + small:
        copy.wait_send()
    for k in range(7):
        block = blocks.at[8 * (1 - core) + sources[k]]
        for i in range(4):
            part = block.at[quarter(turn(x, i, 4))]
            remote(part, part, c_send.at[4 * k + i], c_recv.at[4 * k + i], twin).wait_recv()
    block = blocks.at[8 * (1 - core) + group]
    remote(block, block, c_send.at[28], c_recv.at[28], twin).wait_recv()

    bounds = [table[STARTS + index, 0] for index in range(N_DOCS - 1)]
    low = lax.broadcasted_iota(I32, (WIDTH, TOK), 1) < RUN
    bases = [table[me, RUN * run] for run in range(2)]
    tops = [base // TOK - (SLOTS - 1) for base in bases]

    for run in range(2):
        for slot in range(SLOTS):
            tile = jnp.clip(tops[run] + slot, 0, N_CTX - 1)
            one, two = (jnp.clip(table[INVERSE, 2 * tile + i], 0, N_CTX - 1) for i in range(2))
            keys[run, :, TOK * slot : TOK * (slot + 1)] = jnp.where(low, blocks[one], blocks[two])

        position = bases[run] + lax.broadcasted_iota(I32, (ROWS, 1), 0) % RUN
        begin = jnp.zeros((ROWS, 1), I32)
        for bound in bounds:
            begin = jnp.where(position >= bound, bound, begin)
        begin = begin - tops[run] * TOK
        position = position - tops[run] * TOK

        peak = jnp.full((ROWS, TOK), -1e30, F32)
        for start in range(0, SPAN, 2 * TOK):
            size = min(2 * TOK, SPAN - start)
            columns = slice(start, start + size)
            key = start + lax.broadcasted_iota(I32, (ROWS, size), 1)
            allowed = key >= begin
            if start + size == SPAN:
                allowed = allowed & (key <= position)
            value = jnp.where(allowed, dot(q_rows[run], keys[run, :, columns]), -1e30)
            score[:, columns] = value
            grad_p[:, columns] = dot(g_rows[run], keys[run, :LAT, columns])
            for part in range(size // TOK):
                peak = jnp.maximum(peak, value[:, TOK * part : TOK * (part + 1)])
        peak = jnp.max(peak, axis=1, keepdims=True) * (SCALE * LOG2E)

        sums = jnp.zeros((ROWS, TOK), F32)
        mixed = jnp.zeros((ROWS, TOK), F32)
        for slot in range(SLOTS):
            columns = slice(TOK * slot, TOK * (slot + 1))
            weight = jnp.exp2(score[:, columns] * (SCALE * LOG2E) - peak)
            score[:, columns] = weight
            sums = sums + weight
            mixed = mixed + weight * grad_p[:, columns]
        inverse = 1.0 / jnp.sum(sums, axis=1, keepdims=True)
        delta = jnp.sum(mixed, axis=1, keepdims=True) * inverse
        scaled = inverse * SCALE
        for slot in range(SLOTS):
            columns = slice(TOK * slot, TOK * (slot + 1))
            weight = score[:, columns]
            prob[run, :, columns] = (weight * inverse).astype(BF16)
            grad_s[run, :, columns] = (weight * scaled * (grad_p[:, columns] - delta)).astype(BF16)

    def gradient(rows, target):
        size = rows.stop - rows.start
        values = slice(rows.start, min(rows.stop, LAT))
        for run in range(2):
            for start in range(0, SPAN, 2 * TOK):
                width = min(2 * TOK, SPAN - start)
                columns = slice(start, start + width)
                both = dot(q_cols[run, rows, :], grad_s[run, :, columns])
                value = dot(g_cols[run, values, :], prob[run, :, columns])
                if values.stop < rows.stop:
                    value = jnp.concatenate(
                        [value, jnp.zeros((rows.stop - values.stop, width), F32)], axis=0
                    )
                both = both + value
                for part in range(width // TOK):
                    dkv[run, start // TOK + part, :size] = both[:, TOK * part : TOK * (part + 1)]
        first_lanes = lax.broadcasted_iota(I32, (size, TOK), 1) < RUN
        for device in range(N_CTX):
            out = []
            runs = [table[device, RUN * half] // RUN for half in range(2)]
            for parity in range(2):
                tile = jnp.where(runs[0] % 2 == parity, runs[0], runs[1]) // 2
                found = []
                for run in range(2):
                    slot = tile - tops[run]
                    inside = (slot >= 0) & (slot < SLOTS)
                    found.append(dkv[run, jnp.where(inside, slot, SLOTS), :size])
                out.append(found[0] + found[1])
            target[device // 8, device % 8] = jnp.where(first_lanes, out[0], out[1]).astype(BF16)

    def query_gradient(run):
        dq[run] = dot_nt(grad_s[run], keys[run])

    def rows_of(index, size):
        return pl.ds(pl.multiple_of(size * index, 16), size)

    swaps, x_step, y_step = [], [], []
    chip = [x_part0, y_part0, x_part1, y_part1]
    twin_part = [x_twin0, y_twin0, x_twin1, y_twin1]
    x_recv = [x_recv0, x_recv1]
    y_recv = [y_recv0, y_recv1]

    def to_twin_core(c):
        copy = remote(chip[c].at[1 - core], twin_part[c], t_send.at[c], t_recv.at[c], twin)
        copy.start()
        swaps.append(copy)

    def over_links(c):
        swaps[c].wait_recv()
        ours = chip[c]
        for g in range(8):
            ours[core, g] = (ours[core, g].astype(F32) + twin_part[c][g].astype(F32)).astype(BF16)
        half = c // 2
        if c % 2 == 0:
            size = X_SIZES[half]
            for k in range(3):
                source = ours.at[core, :, rows_of(turn(x, k + 1, 4), size)]
                at = 3 * half + k
                copy = remote(source, x_recv[half].at[k], x_send.at[at], x_got.at[at], along_x(k + 1))
                copy.start()
                x_step.append(copy)
        else:
            for k in range(7):
                source = ours.at[core, targets[k]]
                at = 7 * half + k
                copy = remote(source, y_recv[half].at[k], y_send.at[at], y_got.at[at], mates[k])
                copy.start()
                y_step.append(copy)

    dkv[:, SLOTS] = jnp.zeros((2, CHUNK, TOK), F32)
    for c in range(4):
        gradient(slice(BASES[c], BASES[c + 1]), chip[c])
        to_twin_core(c)
        if c:
            over_links(c - 1)
    over_links(3)

    for run in range(2):
        query_gradient(run)
    for h in range(HEADS):
        rows = slice(RUN * h, RUN * (h + 1))
        both = jnp.concatenate([dq[0, rows, :], dq[1, rows, :]], axis=0)
        q_in[h] = both.T.astype(BF16)
    store = pltpu.make_async_copy(q_in, d_query, in_sem.at[2])
    store.start()

    for copy in x_step:
        copy.wait_recv()
    for half in range(2):
        size, first_row = X_SIZES[half], half * X_SIZES[0]
        for g in range(8):
            total = chip[2 * half][core, g, rows_of(x, size), :].astype(F32)
            for k in range(3):
                total = total + x_recv[half][k, g].astype(F32)
            x_sum[g, first_row : first_row + size] = total.astype(BF16)
    def window(index):
        return pl.ds(pl.multiple_of(X_SIZES[0] * index, 16), X_PIECE)

    x_end = []
    for k, device in enumerate(plane):
        source = x_sum.at[turn(group, (k + 1) % 8, 8), window(turn(low_z, (k + 1) // 8, 2))]
        copy = remote(source, x_last.at[k], xl_send.at[k], xl_got.at[k], device)
        copy.start()
        x_end.append(copy)
    for copy in y_step:
        copy.wait_recv()
    for half in range(2):
        total = chip[2 * half + 1][core, group].astype(F32)
        for k in range(7):
            total = total + y_recv[half][k].astype(F32)
        y_sum[half] = total.astype(BF16)
    y_end = []
    for k, device in enumerate(over_tp):
        other = turn(tp, k + 1, N_TP)
        source = y_sum.at[lax.rem(other, 2), rows_of(other // 2, Y_SIZE)]
        copy = remote(source, y_last.at[k], yl_send.at[k], yl_got.at[k], device)
        copy.start()
        y_end.append(copy)

    for copy in x_end:
        copy.wait_recv()
    total = x_sum[group, window(low_z), :].astype(F32)
    for k in range(15):
        total = total + x_last[k].astype(F32)
    piece[:X_PIECE] = total.astype(BF16)
    for copy in y_end:
        copy.wait_recv()
    total = y_sum[low_z, rows_of(x, Y_SIZE), :].astype(F32)
    for k in range(7):
        total = total + y_last[k].astype(F32)
    piece[X_PIECE:] = total.astype(BF16)
    keep = pltpu.make_async_copy(piece, pieces.at[tp], in_sem.at[0])
    keep.start()
    out_step = []
    for k, device in enumerate(over_tp):
        copy = remote(piece, pieces.at[tp], o_send.at[k], o_recv.at[k], device)
        copy.start()
        out_step.append(copy)
    for k, device in enumerate(over_tp):
        other = pieces.at[turn(tp, -(k + 1), N_TP)]
        remote(other, other, o_send.at[k], o_recv.at[k], device).wait_recv()
    keep.wait()
    store.wait()
    for copy in swaps + x_step + y_step + x_end + y_end + out_step:
        copy.wait_send()


def even_first(value, here):
    swapped = jnp.broadcast_to(here[:, :1] // RUN % 2 == 1, value.shape)
    value = value.astype(F32)
    return jnp.where(swapped, pltpu.roll(value, RUN, 1), value).astype(BF16)


def finish(d_query, pieces, positions, query_out, latent_out, held, parts, place, whole, in_sem, out_sem):
    loads = [
        pltpu.make_async_copy(pieces, parts, in_sem.at[HEADS]),
        pltpu.make_async_copy(positions, place, in_sem.at[HEADS + 1]),
    ]
    for h in range(HEADS):
        loads.append(pltpu.make_async_copy(d_query.at[h], held.at[h], in_sem.at[h]))
    for copy in loads:
        copy.start()
    stores = []
    for h in range(HEADS):
        loads[2 + h].wait()
        stores.append(pltpu.make_async_copy(held.at[h], query_out.at[h], out_sem.at[h]))
        stores[-1].start()
    loads[0].wait()
    loads[1].wait()
    for x in range(N_TP // 2):
        for low_z in range(2):
            size = X_SIZES[low_z]
            at = BASES[2 * low_z] + size * x
            whole[at : at + size, :] = parts[2 * x + low_z, :size]
            at = BASES[2 * low_z + 1] + Y_SIZE * x
            whole[at : at + Y_SIZE, :] = parts[2 * x + low_z, X_PIECE:]
    whole[...] = even_first(whole[...], place[...])
    stores.append(pltpu.make_async_copy(whole, latent_out, out_sem.at[HEADS]))
    stores[-1].start()
    for copy in stores:
        copy.wait()


def local(query, latent, d_out, positions, doc_ids):
    whole = pl.BlockSpec(memory_space=pl.ANY)
    vmem, dma = pltpu.VMEM, pltpu.SemaphoreType.DMA
    here = positions.reshape(1, TOK)
    d_query, pieces = pl.pallas_call(
        kernel,
        out_shape=[
            jax.ShapeDtypeStruct((HEADS, WIDTH, TOK), BF16),
            jax.ShapeDtypeStruct((N_TP, PIECE, TOK), BF16),
        ],
        in_specs=[whole] * 5,
        out_specs=[whole, whole],
        scratch_shapes=[
            vmem((HEADS, WIDTH, TOK), BF16),
            vmem((TOK * HEADS, LAT), BF16),
            vmem((LAT // 128, TOK * HEADS, 128), F32),
            vmem((2, ROWS, WIDTH), BF16),
            vmem((2, WIDTH, ROWS), BF16),
            vmem((2, ROWS, LAT), BF16),
            vmem((2, LAT, ROWS), BF16),
            vmem((N_CTX, WIDTH, TOK), BF16),
            vmem((2, 8, 1, TOK), I32),
            vmem((24, TOK), I32),
            pltpu.SMEM((24, TOK), I32),
            vmem((2, WIDTH, SPAN), BF16),
            vmem((ROWS, SPAN), F32),
            vmem((ROWS, SPAN), F32),
            vmem((2, ROWS, SPAN), BF16),
            vmem((2, ROWS, SPAN), BF16),
            vmem((2, SLOTS + 1, CHUNK, TOK), F32),
            vmem((2, ROWS, WIDTH), F32),
        ]
        + [vmem((2, 8, BASES[c + 1] - BASES[c], TOK), BF16) for c in range(4)]
        + [vmem((8, BASES[c + 1] - BASES[c], TOK), BF16) for c in range(4)]
        + [
            vmem((3, 8, X_SIZES[0], TOK), BF16),
            vmem((7, 4 * Y_SIZE, TOK), BF16),
            vmem((3, 8, X_SIZES[1], TOK), BF16),
            vmem((7, 4 * Y_SIZE, TOK), BF16),
            vmem((8, X_BOTH, TOK), BF16),
            vmem((2, 4 * Y_SIZE, TOK), BF16),
            vmem((15, X_PIECE, TOK), BF16),
            vmem((7, Y_SIZE, TOK), BF16),
            vmem((PIECE, TOK), BF16),
            vmem((WIDTH, TOK), BF16),
            vmem((N_CTX, TOK), I32),
            dma((5,)),
            dma,
        ]
        + [dma((size,)) for size in (14, 14, 29, 8, 4, 6, 14, 15, 7, 7) for _ in range(2)],
        compiler_params=pltpu.CompilerParams(
            collective_id=0, has_side_effects=True, vmem_limit_bytes=63 << 20
        ),
        name="latent_attention_backward",
    )(
        latent.T,
        here,
        doc_ids.reshape(-1, TOK),
        query.transpose(1, 2, 0),
        d_out.reshape(TOK * HEADS, LAT),
    )
    d_query, d_latent = pl.pallas_call(
        finish,
        out_shape=[
            jax.ShapeDtypeStruct((HEADS, WIDTH, TOK), BF16),
            jax.ShapeDtypeStruct((WIDTH, TOK), BF16),
        ],
        in_specs=[whole] * 3,
        out_specs=[whole] * 2,
        scratch_shapes=[
            vmem((HEADS, WIDTH, TOK), BF16),
            vmem((N_TP, PIECE, TOK), BF16),
            vmem((1, TOK), I32),
            vmem((WIDTH, TOK), BF16),
            dma((HEADS + 2,)),
            dma((HEADS + 1,)),
        ],
        compiler_params=pltpu.CompilerParams(vmem_limit_bytes=63 << 20),
        name="finish",
    )(d_query, pieces, here)
    return (d_query.transpose(2, 0, 1), d_latent.T)


def solution(mesh):
    return jax.shard_map(
        local,
        mesh=mesh,
        in_specs=(P("ctx", "tp", None), P("ctx", None), P("ctx", "tp", None), P("ctx"), P()),
        out_specs=(P("ctx", "tp", None), P("ctx", None)),
        check_vma=False,
    )
```

```python
import jax
import jax.numpy as jnp
from jax import lax
from jax.experimental import pallas as pl
from jax.experimental.pallas import tpu as pltpu
from jax.sharding import PartitionSpec as P

MESH = pl.DeviceIdType.MESH
F32, BF16, I32 = jnp.float32, jnp.bfloat16, jnp.int32
SCALE = 192.0 ** (-0.5)
LOG2E = 1.4426950408889634
WIDTH, LAT, TOK, HEADS, RUN = 576, 512, 128, 8, 64
ROWS = HEADS * RUN
N_CTX, N_TP, N_DOCS = 16, 8, 4
SLOTS = 9
SPAN = SLOTS * TOK
QUARTER = WIDTH // 4
X_SIZES, Y_SIZE = (32, 48), 32
X_BOTH, X_PIECE, PIECE = 80, 48, 80
BASES = (0, 128, 256, 448, 576)
CHUNK = 192
INVERSE, STARTS = N_CTX, N_CTX + 1


def dot(left, right):
    return jnp.dot(left, right, preferred_element_type=F32)


def dot_nt(left, right):
    return lax.dot_general(left, right, (((1,), (1,)), ((), ())), preferred_element_type=F32)


def remote(src, dst, send, recv, device):
    return pltpu.make_async_remote_copy(
        src_ref=src, dst_ref=dst, send_sem=send, recv_sem=recv, device_id=device, device_id_type=MESH
    )


def kernel(
    latent, positions, docs, query, d_out, d_query, pieces,
    q_in, g_in, g_wide, q_rows, q_cols, g_rows, g_cols, blocks, places, info, table,
    keys, score, grad_p, prob, grad_s, dkv, dq,
    x_part0, y_part0, x_part1, y_part1, x_twin0, y_twin0, x_twin1, y_twin1,
    x_recv0, y_recv0, x_recv1, y_recv1, x_sum, y_sum,
    x_last, y_last, piece, raw, docs_in,
    in_sem, info_sem, a_send, a_recv, b_send, b_recv, c_send, c_recv, pos_send, pos_recv,
    t_send, t_recv, x_send, x_got, y_send, y_got, xl_send, xl_got, yl_send, yl_got, o_send, o_recv,
):
    ctx, tp = lax.axis_index("ctx"), lax.axis_index("tp")
    core, group = lax.rem(ctx, 2), ctx // 2
    x, low_z = tp // 2, lax.rem(tp, 2)

    def turn(index, step, size):
        return lax.rem(index + step + size, size)

    def along_x(step):
        return (ctx, 2 * turn(x, step, 4) + low_z)

    y, high_z = group // 2, lax.rem(group, 2)
    me = 8 * core + group
    twin = (2 * group + 1 - core, tp)
    mates, targets, sources = [], [], []
    for k in range(1, 8):
        flip, step = k // 4, k % 4
        over = 1 - high_z if flip else high_z
        targets.append(2 * turn(y, step, 4) + over)
        sources.append(2 * turn(y, -step, 4) + over)
        mates.append((2 * targets[-1] + core, 2 * x + (1 - low_z if flip else low_z)))
    over_tp = [(ctx, turn(tp, k, N_TP)) for k in range(1, N_TP)]
    plane = [
        (2 * turn(group, k, 8) + core, 2 * x + turn(low_z, j, 2))
        for j in range(2) for k in range(8) if j or k
    ]

    friends = mates + [twin, along_x(1), along_x(-1), plane[7]]
    barrier = pltpu.get_barrier_semaphore()
    for device in friends:
        pl.semaphore_signal(barrier, inc=1, device_id=device, device_id_type=MESH)
    loads = [
        pltpu.make_async_copy(positions, places.at[core, group], in_sem.at[3]),
        pltpu.make_async_copy(latent, raw, in_sem.at[0]),
        pltpu.make_async_copy(query, q_in, in_sem.at[1]),
        pltpu.make_async_copy(d_out, g_in, in_sem.at[2]),
        pltpu.make_async_copy(docs, docs_in, in_sem.at[4]),
    ]
    for copy in loads:
        copy.start()
    loads[0].wait()
    loads[1].wait()
    blocks[me] = even_first(raw[...], places[core, group])
    pl.semaphore_wait(barrier, len(friends))

    def quarter(index):
        return pl.ds(pl.multiple_of(QUARTER * index, 16), QUARTER)

    first, small = [], []
    for turn_of in range(2):
        for k, device in enumerate(mates):
            j = (turn_of + k) % 2
            part = blocks.at[me, quarter(turn(x, j, 4))]
            copy = remote(part, part, a_send.at[2 * k + j], a_recv.at[2 * k + j], device)
            copy.start()
            first.append(copy)
    for k, device in enumerate(mates):
        here = places.at[core, group]
        copy = remote(here, here, pos_send.at[k], pos_recv.at[k], device)
        copy.start()
        small.append(copy)
    to_twin = [remote(blocks.at[me], blocks.at[me], c_send.at[28], c_recv.at[28], twin)]
    to_twin[0].start()

    loads[2].wait()
    for h in range(HEADS):
        rows = q_in[h].T
        for run in range(2):
            q_rows[run, RUN * h : RUN * (h + 1), :] = rows[RUN * run : RUN * (run + 1)]

    def share(k, i, block, index):
        part = block.at[quarter(index)]
        copy = remote(part, part, c_send.at[4 * k + i], c_recv.at[4 * k + i], twin)
        copy.start()
        to_twin.append(copy)

    second = []
    for turn_of in range(2):
        for k in range(7):
            j = (turn_of + k) % 2
            block = blocks.at[8 * core + sources[k]]
            part = block.at[quarter(turn(x, j, 4))]
            at = 2 * k + j
            remote(part, part, a_send.at[at], a_recv.at[at], mates[k]).wait_recv()
            copy = remote(part, part, b_send.at[at], b_recv.at[at], along_x(1 - 2 * j))
            copy.start()
            second.append(copy)
            share(k, j, block, turn(x, j, 4))
    for k in range(7):
        here = places.at[core, sources[k]]
        remote(here, here, pos_send.at[k], pos_recv.at[k], mates[k]).wait_recv()
    here = places.at[core]
    copy = remote(here, here, pos_send.at[7], pos_recv.at[7], twin)
    copy.start()
    small.append(copy)

    for run in range(2):
        for part in range(ROWS // 128):
            pair = slice(128 * part, 128 * (part + 1))
            q_cols[run, :, pair] = q_rows[run, pair, :].T
    loads[3].wait()
    for part in range(LAT // 128):
        lanes = slice(128 * part, 128 * (part + 1))
        g_wide[part] = g_in[:, lanes].astype(F32)
        for h in range(HEADS):
            rows = g_wide[part, pl.ds(h, TOK, HEADS), :].astype(BF16)
            for run in range(2):
                g_rows[run, RUN * h : RUN * (h + 1), lanes] = rows[RUN * run : RUN * (run + 1)]
    for run in range(2):
        for part in range(ROWS // 128):
            pair = slice(128 * part, 128 * (part + 1))
            g_cols[run, :, pair] = g_rows[run, pair, :].T

    here = places.at[1 - core]
    remote(here, here, pos_send.at[7], pos_recv.at[7], twin).wait_recv()
    lane = lax.broadcasted_iota(I32, (N_CTX, TOK), 1)
    row = lax.broadcasted_iota(I32, (N_CTX, TOK), 0)
    at = jnp.concatenate([places[d // 8, d % 8] for d in range(N_CTX)], axis=0)
    one, two = at[:, :1] // RUN, at[:, RUN : RUN + 1] // RUN
    holder = jnp.where((one == lane) | (two == lane), row, 0)
    info[:N_CTX] = at
    info[INVERSE : INVERSE + 1] = jnp.sum(holder, axis=0, keepdims=True)
    loads[4].wait()
    for value in range(1, N_DOCS):
        count = jnp.sum((docs_in[...] < value).astype(I32), keepdims=True)
        info[STARTS + value - 1 : STARTS + value] = jnp.broadcast_to(count, (1, TOK))
    copy = pltpu.make_async_copy(info, table, info_sem)
    copy.start()
    copy.wait()

    for turn_of in range(2):
        for k in range(7):
            j = (turn_of + k) % 2
            block = blocks.at[8 * core + sources[k]]
            part = block.at[quarter(turn(x, 3 - j, 4))]
            at = 2 * k + j
            remote(part, part, b_send.at[at], b_recv.at[at], along_x(1 - 2 * j)).wait_recv()
            share(k, 3 - j, block, turn(x, 3 - j, 4))
    for copy in first + second + to_twin + small:
        copy.wait_send()
    for k in range(7):
        block = blocks.at[8 * (1 - core) + sources[k]]
        for i in range(4):
            part = block.at[quarter(turn(x, i, 4))]
            remote(part, part, c_send.at[4 * k + i], c_recv.at[4 * k + i], twin).wait_recv()
    block = blocks.at[8 * (1 - core) + group]
    remote(block, block, c_send.at[28], c_recv.at[28], twin).wait_recv()

    bounds = [table[STARTS + index, 0] for index in range(N_DOCS - 1)]
    low = lax.broadcasted_iota(I32, (WIDTH, TOK), 1) < RUN
    bases = [table[me, RUN * run] for run in range(2)]
    tops = [base // TOK - (SLOTS - 1) for base in bases]

    for run in range(2):
        for slot in range(SLOTS):
            tile = jnp.clip(tops[run] + slot, 0, N_CTX - 1)
            one, two = (jnp.clip(table[INVERSE, 2 * tile + i], 0, N_CTX - 1) for i in range(2))
            keys[run, :, TOK * slot : TOK * (slot + 1)] = jnp.where(low, blocks[one], blocks[two])

        position = bases[run] + lax.broadcasted_iota(I32, (ROWS, 1), 0) % RUN
        begin = jnp.zeros((ROWS, 1), I32)
        for bound in bounds:
            begin = jnp.where(position >= bound, bound, begin)
        begin = begin - tops[run] * TOK
        position = position - tops[run] * TOK

        peak = jnp.full((ROWS, TOK), -1e30, F32)
        for start in range(0, SPAN, 2 * TOK):
            size = min(2 * TOK, SPAN - start)
            columns = slice(start, start + size)
            key = start + lax.broadcasted_iota(I32, (ROWS, size), 1)
            allowed = key >= begin
            if start + size == SPAN:
                allowed = allowed & (key <= position)
            value = jnp.where(allowed, dot(q_rows[run], keys[run, :, columns]), -1e30)
            score[:, columns] = value
            grad_p[:, columns] = dot(g_rows[run], keys[run, :LAT, columns])
            for part in range(size // TOK):
                peak = jnp.maximum(peak, value[:, TOK * part : TOK * (part + 1)])
        peak = jnp.max(peak, axis=1, keepdims=True) * (SCALE * LOG2E)

        sums = jnp.zeros((ROWS, TOK), F32)
        mixed = jnp.zeros((ROWS, TOK), F32)
        for slot in range(SLOTS):
            columns = slice(TOK * slot, TOK * (slot + 1))
            weight = jnp.exp2(score[:, columns] * (SCALE * LOG2E) - peak)
            score[:, columns] = weight
            sums = sums + weight
            mixed = mixed + weight * grad_p[:, columns]
        inverse = 1.0 / jnp.sum(sums, axis=1, keepdims=True)
        delta = jnp.sum(mixed, axis=1, keepdims=True) * inverse
        scaled = inverse * SCALE
        for slot in range(SLOTS):
            columns = slice(TOK * slot, TOK * (slot + 1))
            weight = score[:, columns]
            prob[run, :, columns] = (weight * inverse).astype(BF16)
            grad_s[run, :, columns] = (weight * scaled * (grad_p[:, columns] - delta)).astype(BF16)

    def gradient(rows, target):
        size = rows.stop - rows.start
        values = slice(rows.start, min(rows.stop, LAT))
        for run in range(2):
            for start in range(0, SPAN, 2 * TOK):
                width = min(2 * TOK, SPAN - start)
                columns = slice(start, start + width)
                both = dot(q_cols[run, rows, :], grad_s[run, :, columns])
                value = dot(g_cols[run, values, :], prob[run, :, columns])
                if values.stop < rows.stop:
                    value = jnp.concatenate(
                        [value, jnp.zeros((rows.stop - values.stop, width), F32)], axis=0
                    )
                both = both + value
                for part in range(width // TOK):
                    dkv[run, start // TOK + part, :size] = both[:, TOK * part : TOK * (part + 1)]
        first_lanes = lax.broadcasted_iota(I32, (size, TOK), 1) < RUN
        for device in range(N_CTX):
            out = []
            runs = [table[device, RUN * half] // RUN for half in range(2)]
            for parity in range(2):
                tile = jnp.where(runs[0] % 2 == parity, runs[0], runs[1]) // 2
                found = []
                for run in range(2):
                    slot = tile - tops[run]
                    inside = (slot >= 0) & (slot < SLOTS)
                    found.append(dkv[run, jnp.where(inside, slot, SLOTS), :size])
                out.append(found[0] + found[1])
            target[device // 8, device % 8] = jnp.where(first_lanes, out[0], out[1]).astype(BF16)

    def query_gradient(run):
        dq[run] = dot_nt(grad_s[run], keys[run])

    def rows_of(index, size):
        return pl.ds(pl.multiple_of(size * index, 16), size)

    swaps, x_step, y_step = [], [], []
    chip = [x_part0, y_part0, x_part1, y_part1]
    twin_part = [x_twin0, y_twin0, x_twin1, y_twin1]
    x_recv = [x_recv0, x_recv1]
    y_recv = [y_recv0, y_recv1]

    def to_twin_core(c):
        copy = remote(chip[c].at[1 - core], twin_part[c], t_send.at[c], t_recv.at[c], twin)
        copy.start()
        swaps.append(copy)

    def over_links(c):
        swaps[c].wait_recv()
        ours = chip[c]
        for g in range(8):
            ours[core, g] = (ours[core, g].astype(F32) + twin_part[c][g].astype(F32)).astype(BF16)
        half = c // 2
        if c % 2 == 0:
            size = X_SIZES[half]
            for k in range(3):
                source = ours.at[core, :, rows_of(turn(x, k + 1, 4), size)]
                at = 3 * half + k
                copy = remote(source, x_recv[half].at[k], x_send.at[at], x_got.at[at], along_x(k + 1))
                copy.start()
                x_step.append(copy)
        else:
            for k in range(7):
                source = ours.at[core, targets[k]]
                at = 7 * half + k
                copy = remote(source, y_recv[half].at[k], y_send.at[at], y_got.at[at], mates[k])
                copy.start()
                y_step.append(copy)

    dkv[:, SLOTS] = jnp.zeros((2, CHUNK, TOK), F32)
    for c in range(4):
        gradient(slice(BASES[c], BASES[c + 1]), chip[c])
        to_twin_core(c)
        if c:
            over_links(c - 1)
    over_links(3)

    for run in range(2):
        query_gradient(run)
    for h in range(HEADS):
        rows = slice(RUN * h, RUN * (h + 1))
        both = jnp.concatenate([dq[0, rows, :], dq[1, rows, :]], axis=0)
        q_in[h] = both.T.astype(BF16)
    store = pltpu.make_async_copy(q_in, d_query, in_sem.at[2])
    store.start()

    for half in range(2):
        for copy in x_step[3 * half : 3 * half + 3]:
            copy.wait_recv()
        size, first_row = X_SIZES[half], half * X_SIZES[0]
        for g in range(8):
            total = chip[2 * half][core, g, rows_of(x, size), :].astype(F32)
            for k in range(3):
                total = total + x_recv[half][k, g].astype(F32)
            x_sum[g, first_row : first_row + size] = total.astype(BF16)
    def window(index):
        return pl.ds(pl.multiple_of(X_SIZES[0] * index, 16), X_PIECE)

    x_end = []
    for k, device in enumerate(plane):
        source = x_sum.at[turn(group, (k + 1) % 8, 8), window(turn(low_z, (k + 1) // 8, 2))]
        copy = remote(source, x_last.at[k], xl_send.at[k], xl_got.at[k], device)
        copy.start()
        x_end.append(copy)
    for half in range(2):
        for copy in y_step[7 * half : 7 * half + 7]:
            copy.wait_recv()
        total = chip[2 * half + 1][core, group].astype(F32)
        for k in range(7):
            total = total + y_recv[half][k].astype(F32)
        y_sum[half] = total.astype(BF16)
    y_end = []
    for k, device in enumerate(over_tp):
        other = turn(tp, k + 1, N_TP)
        source = y_sum.at[lax.rem(other, 2), rows_of(other // 2, Y_SIZE)]
        copy = remote(source, y_last.at[k], yl_send.at[k], yl_got.at[k], device)
        copy.start()
        y_end.append(copy)

    for copy in x_end:
        copy.wait_recv()
    total = x_sum[group, window(low_z), :].astype(F32)
    for k in range(15):
        total = total + x_last[k].astype(F32)
    piece[:X_PIECE] = total.astype(BF16)
    for copy in y_end:
        copy.wait_recv()
    total = y_sum[low_z, rows_of(x, Y_SIZE), :].astype(F32)
    for k in range(7):
        total = total + y_last[k].astype(F32)
    piece[X_PIECE:] = total.astype(BF16)
    keep = pltpu.make_async_copy(piece, pieces.at[tp], in_sem.at[0])
    keep.start()
    out_step = []
    for k, device in enumerate(over_tp):
        copy = remote(piece, pieces.at[tp], o_send.at[k], o_recv.at[k], device)
        copy.start()
        out_step.append(copy)
    for k, device in enumerate(over_tp):
        other = pieces.at[turn(tp, -(k + 1), N_TP)]
        remote(other, other, o_send.at[k], o_recv.at[k], device).wait_recv()
    keep.wait()
    store.wait()
    for copy in swaps + x_step + y_step + x_end + y_end + out_step:
        copy.wait_send()


def even_first(value, here):
    swapped = jnp.broadcast_to(here[:, :1] // RUN % 2 == 1, value.shape)
    value = value.astype(F32)
    return jnp.where(swapped, pltpu.roll(value, RUN, 1), value).astype(BF16)


def finish(d_query, pieces, positions, query_out, latent_out, held, parts, place, whole, in_sem, out_sem):
    loads = [
        pltpu.make_async_copy(pieces, parts, in_sem.at[HEADS]),
        pltpu.make_async_copy(positions, place, in_sem.at[HEADS + 1]),
    ]
    for h in range(HEADS):
        loads.append(pltpu.make_async_copy(d_query.at[h], held.at[h], in_sem.at[h]))
    for copy in loads:
        copy.start()
    stores = []
    for h in range(HEADS):
        loads[2 + h].wait()
        stores.append(pltpu.make_async_copy(held.at[h], query_out.at[h], out_sem.at[h]))
        stores[-1].start()
    loads[0].wait()
    loads[1].wait()
    for x in range(N_TP // 2):
        for low_z in range(2):
            size = X_SIZES[low_z]
            at = BASES[2 * low_z] + size * x
            whole[at : at + size, :] = parts[2 * x + low_z, :size]
            at = BASES[2 * low_z + 1] + Y_SIZE * x
            whole[at : at + Y_SIZE, :] = parts[2 * x + low_z, X_PIECE:]
    whole[...] = even_first(whole[...], place[...])
    stores.append(pltpu.make_async_copy(whole, latent_out, out_sem.at[HEADS]))
    stores[-1].start()
    for copy in stores:
        copy.wait()


def local(query, latent, d_out, positions, doc_ids):
    whole = pl.BlockSpec(memory_space=pl.ANY)
    vmem, dma = pltpu.VMEM, pltpu.SemaphoreType.DMA
    here = positions.reshape(1, TOK)
    d_query, pieces = pl.pallas_call(
        kernel,
        out_shape=[
            jax.ShapeDtypeStruct((HEADS, WIDTH, TOK), BF16),
            jax.ShapeDtypeStruct((N_TP, PIECE, TOK), BF16),
        ],
        in_specs=[whole] * 5,
        out_specs=[whole, whole],
        scratch_shapes=[
            vmem((HEADS, WIDTH, TOK), BF16),
            vmem((TOK * HEADS, LAT), BF16),
            vmem((LAT // 128, TOK * HEADS, 128), F32),
            vmem((2, ROWS, WIDTH), BF16),
            vmem((2, WIDTH, ROWS), BF16),
            vmem((2, ROWS, LAT), BF16),
            vmem((2, LAT, ROWS), BF16),
            vmem((N_CTX, WIDTH, TOK), BF16),
            vmem((2, 8, 1, TOK), I32),
            vmem((24, TOK), I32),
            pltpu.SMEM((24, TOK), I32),
            vmem((2, WIDTH, SPAN), BF16),
            vmem((ROWS, SPAN), F32),
            vmem((ROWS, SPAN), F32),
            vmem((2, ROWS, SPAN), BF16),
            vmem((2, ROWS, SPAN), BF16),
            vmem((2, SLOTS + 1, CHUNK, TOK), F32),
            vmem((2, ROWS, WIDTH), F32),
        ]
        + [vmem((2, 8, BASES[c + 1] - BASES[c], TOK), BF16) for c in range(4)]
        + [vmem((8, BASES[c + 1] - BASES[c], TOK), BF16) for c in range(4)]
        + [
            vmem((3, 8, X_SIZES[0], TOK), BF16),
            vmem((7, 4 * Y_SIZE, TOK), BF16),
            vmem((3, 8, X_SIZES[1], TOK), BF16),
            vmem((7, 4 * Y_SIZE, TOK), BF16),
            vmem((8, X_BOTH, TOK), BF16),
            vmem((2, 4 * Y_SIZE, TOK), BF16),
            vmem((15, X_PIECE, TOK), BF16),
            vmem((7, Y_SIZE, TOK), BF16),
            vmem((PIECE, TOK), BF16),
            vmem((WIDTH, TOK), BF16),
            vmem((N_CTX, TOK), I32),
            dma((5,)),
            dma,
        ]
        + [dma((size,)) for size in (14, 14, 29, 8, 4, 6, 14, 15, 7, 7) for _ in range(2)],
        compiler_params=pltpu.CompilerParams(
            collective_id=0, has_side_effects=True, vmem_limit_bytes=63 << 20
        ),
        name="latent_attention_backward",
    )(
        latent.T,
        here,
        doc_ids.reshape(-1, TOK),
        query.transpose(1, 2, 0),
        d_out.reshape(TOK * HEADS, LAT),
    )
    d_query, d_latent = pl.pallas_call(
        finish,
        out_shape=[
            jax.ShapeDtypeStruct((HEADS, WIDTH, TOK), BF16),
            jax.ShapeDtypeStruct((WIDTH, TOK), BF16),
        ],
        in_specs=[whole] * 3,
        out_specs=[whole] * 2,
        scratch_shapes=[
            vmem((HEADS, WIDTH, TOK), BF16),
            vmem((N_TP, PIECE, TOK), BF16),
            vmem((1, TOK), I32),
            vmem((WIDTH, TOK), BF16),
            dma((HEADS + 2,)),
            dma((HEADS + 1,)),
        ],
        compiler_params=pltpu.CompilerParams(vmem_limit_bytes=63 << 20),
        name="finish",
    )(d_query, pieces, here)
    return (d_query.transpose(2, 0, 1), d_latent.T)


def solution(mesh):
    return jax.shard_map(
        local,
        mesh=mesh,
        in_specs=(P("ctx", "tp", None), P("ctx", None), P("ctx", "tp", None), P("ctx"), P()),
        out_specs=(P("ctx", "tp", None), P("ctx", None)),
        check_vma=False,
    )
```

```python
import jax
import jax.numpy as jnp
from jax import lax
from jax.experimental import pallas as pl
from jax.experimental.pallas import tpu as pltpu
from jax.sharding import PartitionSpec as P

MESH = pl.DeviceIdType.MESH
F32, BF16, I32 = jnp.float32, jnp.bfloat16, jnp.int32
SCALE = 192.0 ** (-0.5)
LOG2E = 1.4426950408889634
WIDTH, LAT, TOK, HEADS, RUN = 576, 512, 128, 8, 64
ROWS = HEADS * RUN
N_CTX, N_TP, N_DOCS = 16, 8, 4
SLOTS = 9
SPAN = SLOTS * TOK
QUARTER = WIDTH // 4
X_SIZES, Y_SIZE = (32, 48), 32
X_BOTH, X_PIECE, PIECE = 80, 48, 80
BASES = (0, 128, 256, 448, 576)
CHUNK = 192
INVERSE, STARTS = N_CTX, N_CTX + 1


def dot(left, right):
    return jnp.dot(left, right, preferred_element_type=F32)


def dot_nt(left, right):
    return lax.dot_general(left, right, (((1,), (1,)), ((), ())), preferred_element_type=F32)


def remote(src, dst, send, recv, device):
    return pltpu.make_async_remote_copy(
        src_ref=src, dst_ref=dst, send_sem=send, recv_sem=recv, device_id=device, device_id_type=MESH
    )


def kernel(
    latent, positions, docs, query, d_out, d_query, pieces,
    q_in, g_in, g_wide, q_rows, q_cols, g_rows, g_cols, blocks, places, info, table,
    keys, score, grad_p, prob, grad_s, dkv, dq,
    x_part0, y_part0, x_part1, y_part1, x_twin0, y_twin0, x_twin1, y_twin1,
    x_recv0, y_recv0, x_recv1, y_recv1, x_sum, y_sum,
    x_last, y_last, piece, raw, docs_in,
    in_sem, info_sem, a_send, a_recv, b_send, b_recv, c_send, c_recv, pos_send, pos_recv,
    t_send, t_recv, x_send, x_got, y_send, y_got, xl_send, xl_got, yl_send, yl_got, o_send, o_recv,
):
    ctx, tp = lax.axis_index("ctx"), lax.axis_index("tp")
    core, group = lax.rem(ctx, 2), ctx // 2
    x, low_z = tp // 2, lax.rem(tp, 2)

    def turn(index, step, size):
        return lax.rem(index + step + size, size)

    def along_x(step):
        return (ctx, 2 * turn(x, step, 4) + low_z)

    y, high_z = group // 2, lax.rem(group, 2)
    me = 8 * core + group
    twin = (2 * group + 1 - core, tp)
    mates, targets, sources = [], [], []
    for k in range(1, 8):
        flip, step = k // 4, k % 4
        over = 1 - high_z if flip else high_z
        targets.append(2 * turn(y, step, 4) + over)
        sources.append(2 * turn(y, -step, 4) + over)
        mates.append((2 * targets[-1] + core, 2 * x + (1 - low_z if flip else low_z)))
    over_tp = [(ctx, turn(tp, k, N_TP)) for k in range(1, N_TP)]
    plane = [
        (2 * turn(group, k, 8) + core, 2 * x + turn(low_z, j, 2))
        for j in range(2) for k in range(8) if j or k
    ]

    friends = mates + [twin, along_x(1), along_x(-1), plane[7]]
    barrier = pltpu.get_barrier_semaphore()
    for device in friends:
        pl.semaphore_signal(barrier, inc=1, device_id=device, device_id_type=MESH)
    loads = [
        pltpu.make_async_copy(positions, places.at[core, group], in_sem.at[3]),
        pltpu.make_async_copy(latent, raw, in_sem.at[0]),
        pltpu.make_async_copy(query, q_in, in_sem.at[1]),
        pltpu.make_async_copy(d_out, g_in, in_sem.at[2]),
        pltpu.make_async_copy(docs, docs_in, in_sem.at[4]),
    ]
    for copy in loads[:2]:
        copy.start()
    loads[0].wait()
    loads[1].wait()
    blocks[me] = even_first(raw[...], places[core, group])
    pl.semaphore_wait(barrier, len(friends))

    def quarter(index):
        return pl.ds(pl.multiple_of(QUARTER * index, 16), QUARTER)

    first, small = [], []
    for turn_of in range(2):
        for k, device in enumerate(mates):
            j = (turn_of + k) % 2
            part = blocks.at[me, quarter(turn(x, j, 4))]
            copy = remote(part, part, a_send.at[2 * k + j], a_recv.at[2 * k + j], device)
            copy.start()
            first.append(copy)
    for k, device in enumerate(mates):
        here = places.at[core, group]
        copy = remote(here, here, pos_send.at[k], pos_recv.at[k], device)
        copy.start()
        small.append(copy)
    to_twin = [remote(blocks.at[me], blocks.at[me], c_send.at[28], c_recv.at[28], twin)]
    to_twin[0].start()
    for copy in loads[2:]:
        copy.start()

    loads[2].wait()
    for h in range(HEADS):
        rows = q_in[h].T
        for run in range(2):
            q_rows[run, RUN * h : RUN * (h + 1), :] = rows[RUN * run : RUN * (run + 1)]

    def share(k, i, block, index):
        part = block.at[quarter(index)]
        copy = remote(part, part, c_send.at[4 * k + i], c_recv.at[4 * k + i], twin)
        copy.start()
        to_twin.append(copy)

    second = []
    for turn_of in range(2):
        for k in range(7):
            j = (turn_of + k) % 2
            block = blocks.at[8 * core + sources[k]]
            part = block.at[quarter(turn(x, j, 4))]
            at = 2 * k + j
            remote(part, part, a_send.at[at], a_recv.at[at], mates[k]).wait_recv()
            copy = remote(part, part, b_send.at[at], b_recv.at[at], along_x(1 - 2 * j))
            copy.start()
            second.append(copy)
            share(k, j, block, turn(x, j, 4))
    for k in range(7):
        here = places.at[core, sources[k]]
        remote(here, here, pos_send.at[k], pos_recv.at[k], mates[k]).wait_recv()
    here = places.at[core]
    copy = remote(here, here, pos_send.at[7], pos_recv.at[7], twin)
    copy.start()
    small.append(copy)

    for run in range(2):
        for part in range(ROWS // 128):
            pair = slice(128 * part, 128 * (part + 1))
            q_cols[run, :, pair] = q_rows[run, pair, :].T
    loads[3].wait()
    for part in range(LAT // 128):
        lanes = slice(128 * part, 128 * (part + 1))
        g_wide[part] = g_in[:, lanes].astype(F32)
        for h in range(HEADS):
            rows = g_wide[part, pl.ds(h, TOK, HEADS), :].astype(BF16)
            for run in range(2):
                g_rows[run, RUN * h : RUN * (h + 1), lanes] = rows[RUN * run : RUN * (run + 1)]
    for run in range(2):
        for part in range(ROWS // 128):
            pair = slice(128 * part, 128 * (part + 1))
            g_cols[run, :, pair] = g_rows[run, pair, :].T

    here = places.at[1 - core]
    remote(here, here, pos_send.at[7], pos_recv.at[7], twin).wait_recv()
    lane = lax.broadcasted_iota(I32, (N_CTX, TOK), 1)
    row = lax.broadcasted_iota(I32, (N_CTX, TOK), 0)
    at = jnp.concatenate([places[d // 8, d % 8] for d in range(N_CTX)], axis=0)
    one, two = at[:, :1] // RUN, at[:, RUN : RUN + 1] // RUN
    holder = jnp.where((one == lane) | (two == lane), row, 0)
    info[:N_CTX] = at
    info[INVERSE : INVERSE + 1] = jnp.sum(holder, axis=0, keepdims=True)
    loads[4].wait()
    for value in range(1, N_DOCS):
        count = jnp.sum((docs_in[...] < value).astype(I32), keepdims=True)
        info[STARTS + value - 1 : STARTS + value] = jnp.broadcast_to(count, (1, TOK))
    copy = pltpu.make_async_copy(info, table, info_sem)
    copy.start()
    copy.wait()

    for turn_of in range(2):
        for k in range(7):
            j = (turn_of + k) % 2
            block = blocks.at[8 * core + sources[k]]
            part = block.at[quarter(turn(x, 3 - j, 4))]
            at = 2 * k + j
            remote(part, part, b_send.at[at], b_recv.at[at], along_x(1 - 2 * j)).wait_recv()
            share(k, 3 - j, block, turn(x, 3 - j, 4))
    for copy in first + second + to_twin + small:
        copy.wait_send()
    for k in range(7):
        block = blocks.at[8 * (1 - core) + sources[k]]
        for i in range(4):
            part = block.at[quarter(turn(x, i, 4))]
            remote(part, part, c_send.at[4 * k + i], c_recv.at[4 * k + i], twin).wait_recv()
    block = blocks.at[8 * (1 - core) + group]
    remote(block, block, c_send.at[28], c_recv.at[28], twin).wait_recv()

    bounds = [table[STARTS + index, 0] for index in range(N_DOCS - 1)]
    low = lax.broadcasted_iota(I32, (WIDTH, TOK), 1) < RUN
    bases = [table[me, RUN * run] for run in range(2)]
    tops = [base // TOK - (SLOTS - 1) for base in bases]

    for run in range(2):
        for slot in range(SLOTS):
            tile = jnp.clip(tops[run] + slot, 0, N_CTX - 1)
            one, two = (jnp.clip(table[INVERSE, 2 * tile + i], 0, N_CTX - 1) for i in range(2))
            keys[run, :, TOK * slot : TOK * (slot + 1)] = jnp.where(low, blocks[one], blocks[two])

        position = bases[run] + lax.broadcasted_iota(I32, (ROWS, 1), 0) % RUN
        begin = jnp.zeros((ROWS, 1), I32)
        for bound in bounds:
            begin = jnp.where(position >= bound, bound, begin)
        begin = begin - tops[run] * TOK
        position = position - tops[run] * TOK

        peak = jnp.full((ROWS, TOK), -1e30, F32)
        for start in range(0, SPAN, 2 * TOK):
            size = min(2 * TOK, SPAN - start)
            columns = slice(start, start + size)
            key = start + lax.broadcasted_iota(I32, (ROWS, size), 1)
            allowed = key >= begin
            if start + size == SPAN:
                allowed = allowed & (key <= position)
            value = jnp.where(allowed, dot(q_rows[run], keys[run, :, columns]), -1e30)
            score[:, columns] = value
            grad_p[:, columns] = dot(g_rows[run], keys[run, :LAT, columns])
            for part in range(size // TOK):
                peak = jnp.maximum(peak, value[:, TOK * part : TOK * (part + 1)])
        peak = jnp.max(peak, axis=1, keepdims=True) * (SCALE * LOG2E)

        sums = jnp.zeros((ROWS, TOK), F32)
        mixed = jnp.zeros((ROWS, TOK), F32)
        for slot in range(SLOTS):
            columns = slice(TOK * slot, TOK * (slot + 1))
            weight = jnp.exp2(score[:, columns] * (SCALE * LOG2E) - peak)
            score[:, columns] = weight
            sums = sums + weight
            mixed = mixed + weight * grad_p[:, columns]
        inverse = 1.0 / jnp.sum(sums, axis=1, keepdims=True)
        delta = jnp.sum(mixed, axis=1, keepdims=True) * inverse
        scaled = inverse * SCALE
        for slot in range(SLOTS):
            columns = slice(TOK * slot, TOK * (slot + 1))
            weight = score[:, columns]
            prob[run, :, columns] = (weight * inverse).astype(BF16)
            grad_s[run, :, columns] = (weight * scaled * (grad_p[:, columns] - delta)).astype(BF16)

    def gradient(rows, target):
        size = rows.stop - rows.start
        values = slice(rows.start, min(rows.stop, LAT))
        for run in range(2):
            for start in range(0, SPAN, 2 * TOK):
                width = min(2 * TOK, SPAN - start)
                columns = slice(start, start + width)
                both = dot(q_cols[run, rows, :], grad_s[run, :, columns])
                value = dot(g_cols[run, values, :], prob[run, :, columns])
                if values.stop < rows.stop:
                    value = jnp.concatenate(
                        [value, jnp.zeros((rows.stop - values.stop, width), F32)], axis=0
                    )
                both = both + value
                for part in range(width // TOK):
                    dkv[run, start // TOK + part, :size] = both[:, TOK * part : TOK * (part + 1)]
        first_lanes = lax.broadcasted_iota(I32, (size, TOK), 1) < RUN
        for device in range(N_CTX):
            out = []
            runs = [table[device, RUN * half] // RUN for half in range(2)]
            for parity in range(2):
                tile = jnp.where(runs[0] % 2 == parity, runs[0], runs[1]) // 2
                found = []
                for run in range(2):
                    slot = tile - tops[run]
                    inside = (slot >= 0) & (slot < SLOTS)
                    found.append(dkv[run, jnp.where(inside, slot, SLOTS), :size])
                out.append(found[0] + found[1])
            target[device // 8, device % 8] = jnp.where(first_lanes, out[0], out[1]).astype(BF16)

    def query_gradient(run):
        dq[run] = dot_nt(grad_s[run], keys[run])

    def rows_of(index, size):
        return pl.ds(pl.multiple_of(size * index, 16), size)

    swaps, x_step, y_step = [], [], []
    chip = [x_part0, y_part0, x_part1, y_part1]
    twin_part = [x_twin0, y_twin0, x_twin1, y_twin1]
    x_recv = [x_recv0, x_recv1]
    y_recv = [y_recv0, y_recv1]

    def to_twin_core(c):
        copy = remote(chip[c].at[1 - core], twin_part[c], t_send.at[c], t_recv.at[c], twin)
        copy.start()
        swaps.append(copy)

    def over_links(c):
        swaps[c].wait_recv()
        ours = chip[c]
        for g in range(8):
            ours[core, g] = (ours[core, g].astype(F32) + twin_part[c][g].astype(F32)).astype(BF16)
        half = c // 2
        if c % 2 == 0:
            size = X_SIZES[half]
            for k in range(3):
                source = ours.at[core, :, rows_of(turn(x, k + 1, 4), size)]
                at = 3 * half + k
                copy = remote(source, x_recv[half].at[k], x_send.at[at], x_got.at[at], along_x(k + 1))
                copy.start()
                x_step.append(copy)
        else:
            for k in range(7):
                source = ours.at[core, targets[k]]
                at = 7 * half + k
                copy = remote(source, y_recv[half].at[k], y_send.at[at], y_got.at[at], mates[k])
                copy.start()
                y_step.append(copy)

    dkv[:, SLOTS] = jnp.zeros((2, CHUNK, TOK), F32)
    for c in range(4):
        gradient(slice(BASES[c], BASES[c + 1]), chip[c])
        to_twin_core(c)
        if c:
            over_links(c - 1)
    over_links(3)

    for run in range(2):
        query_gradient(run)
    for h in range(HEADS):
        rows = slice(RUN * h, RUN * (h + 1))
        both = jnp.concatenate([dq[0, rows, :], dq[1, rows, :]], axis=0)
        q_in[h] = both.T.astype(BF16)
    store = pltpu.make_async_copy(q_in, d_query, in_sem.at[2])
    store.start()

    for copy in x_step:
        copy.wait_recv()
    for half in range(2):
        size, first_row = X_SIZES[half], half * X_SIZES[0]
        for g in range(8):
            total = chip[2 * half][core, g, rows_of(x, size), :].astype(F32)
            for k in range(3):
                total = total + x_recv[half][k, g].astype(F32)
            x_sum[g, first_row : first_row + size] = total.astype(BF16)
    def window(index):
        return pl.ds(pl.multiple_of(X_SIZES[0] * index, 16), X_PIECE)

    x_end = []
    for k, device in enumerate(plane):
        source = x_sum.at[turn(group, (k + 1) % 8, 8), window(turn(low_z, (k + 1) // 8, 2))]
        copy = remote(source, x_last.at[k], xl_send.at[k], xl_got.at[k], device)
        copy.start()
        x_end.append(copy)
    for copy in y_step:
        copy.wait_recv()
    for half in range(2):
        total = chip[2 * half + 1][core, group].astype(F32)
        for k in range(7):
            total = total + y_recv[half][k].astype(F32)
        y_sum[half] = total.astype(BF16)
    y_end = []
    for k, device in enumerate(over_tp):
        other = turn(tp, k + 1, N_TP)
        source = y_sum.at[lax.rem(other, 2), rows_of(other // 2, Y_SIZE)]
        copy = remote(source, y_last.at[k], yl_send.at[k], yl_got.at[k], device)
        copy.start()
        y_end.append(copy)

    for copy in x_end:
        copy.wait_recv()
    total = x_sum[group, window(low_z), :].astype(F32)
    for k in range(15):
        total = total + x_last[k].astype(F32)
    piece[:X_PIECE] = total.astype(BF16)
    for copy in y_end:
        copy.wait_recv()
    total = y_sum[low_z, rows_of(x, Y_SIZE), :].astype(F32)
    for k in range(7):
        total = total + y_last[k].astype(F32)
    piece[X_PIECE:] = total.astype(BF16)
    keep = pltpu.make_async_copy(piece, pieces.at[tp], in_sem.at[0])
    keep.start()
    out_step = []
    for k, device in enumerate(over_tp):
        copy = remote(piece, pieces.at[tp], o_send.at[k], o_recv.at[k], device)
        copy.start()
        out_step.append(copy)
    for k, device in enumerate(over_tp):
        other = pieces.at[turn(tp, -(k + 1), N_TP)]
        remote(other, other, o_send.at[k], o_recv.at[k], device).wait_recv()
    keep.wait()
    store.wait()
    for copy in swaps + x_step + y_step + x_end + y_end + out_step:
        copy.wait_send()


def even_first(value, here):
    swapped = jnp.broadcast_to(here[:, :1] // RUN % 2 == 1, value.shape)
    value = value.astype(F32)
    return jnp.where(swapped, pltpu.roll(value, RUN, 1), value).astype(BF16)


def finish(d_query, pieces, positions, query_out, latent_out, held, parts, place, whole, in_sem, out_sem):
    loads = [
        pltpu.make_async_copy(pieces, parts, in_sem.at[HEADS]),
        pltpu.make_async_copy(positions, place, in_sem.at[HEADS + 1]),
    ]
    for h in range(HEADS):
        loads.append(pltpu.make_async_copy(d_query.at[h], held.at[h], in_sem.at[h]))
    for copy in loads:
        copy.start()
    stores = []
    for h in range(HEADS):
        loads[2 + h].wait()
        stores.append(pltpu.make_async_copy(held.at[h], query_out.at[h], out_sem.at[h]))
        stores[-1].start()
    loads[0].wait()
    loads[1].wait()
    for x in range(N_TP // 2):
        for low_z in range(2):
            size = X_SIZES[low_z]
            at = BASES[2 * low_z] + size * x
            whole[at : at + size, :] = parts[2 * x + low_z, :size]
            at = BASES[2 * low_z + 1] + Y_SIZE * x
            whole[at : at + Y_SIZE, :] = parts[2 * x + low_z, X_PIECE:]
    whole[...] = even_first(whole[...], place[...])
    stores.append(pltpu.make_async_copy(whole, latent_out, out_sem.at[HEADS]))
    stores[-1].start()
    for copy in stores:
        copy.wait()


def local(query, latent, d_out, positions, doc_ids):
    whole = pl.BlockSpec(memory_space=pl.ANY)
    vmem, dma = pltpu.VMEM, pltpu.SemaphoreType.DMA
    here = positions.reshape(1, TOK)
    d_query, pieces = pl.pallas_call(
        kernel,
        out_shape=[
            jax.ShapeDtypeStruct((HEADS, WIDTH, TOK), BF16),
            jax.ShapeDtypeStruct((N_TP, PIECE, TOK), BF16),
        ],
        in_specs=[whole] * 5,
        out_specs=[whole, whole],
        scratch_shapes=[
            vmem((HEADS, WIDTH, TOK), BF16),
            vmem((TOK * HEADS, LAT), BF16),
            vmem((LAT // 128, TOK * HEADS, 128), F32),
            vmem((2, ROWS, WIDTH), BF16),
            vmem((2, WIDTH, ROWS), BF16),
            vmem((2, ROWS, LAT), BF16),
            vmem((2, LAT, ROWS), BF16),
            vmem((N_CTX, WIDTH, TOK), BF16),
            vmem((2, 8, 1, TOK), I32),
            vmem((24, TOK), I32),
            pltpu.SMEM((24, TOK), I32),
            vmem((2, WIDTH, SPAN), BF16),
            vmem((ROWS, SPAN), F32),
            vmem((ROWS, SPAN), F32),
            vmem((2, ROWS, SPAN), BF16),
            vmem((2, ROWS, SPAN), BF16),
            vmem((2, SLOTS + 1, CHUNK, TOK), F32),
            vmem((2, ROWS, WIDTH), F32),
        ]
        + [vmem((2, 8, BASES[c + 1] - BASES[c], TOK), BF16) for c in range(4)]
        + [vmem((8, BASES[c + 1] - BASES[c], TOK), BF16) for c in range(4)]
        + [
            vmem((3, 8, X_SIZES[0], TOK), BF16),
            vmem((7, 4 * Y_SIZE, TOK), BF16),
            vmem((3, 8, X_SIZES[1], TOK), BF16),
            vmem((7, 4 * Y_SIZE, TOK), BF16),
            vmem((8, X_BOTH, TOK), BF16),
            vmem((2, 4 * Y_SIZE, TOK), BF16),
            vmem((15, X_PIECE, TOK), BF16),
            vmem((7, Y_SIZE, TOK), BF16),
            vmem((PIECE, TOK), BF16),
            vmem((WIDTH, TOK), BF16),
            vmem((N_CTX, TOK), I32),
            dma((5,)),
            dma,
        ]
        + [dma((size,)) for size in (14, 14, 29, 8, 4, 6, 14, 15, 7, 7) for _ in range(2)],
        compiler_params=pltpu.CompilerParams(
            collective_id=0, has_side_effects=True, vmem_limit_bytes=63 << 20
        ),
        name="latent_attention_backward",
    )(
        latent.T,
        here,
        doc_ids.reshape(-1, TOK),
        query.transpose(1, 2, 0),
        d_out.reshape(TOK * HEADS, LAT),
    )
    d_query, d_latent = pl.pallas_call(
        finish,
        out_shape=[
            jax.ShapeDtypeStruct((HEADS, WIDTH, TOK), BF16),
            jax.ShapeDtypeStruct((WIDTH, TOK), BF16),
        ],
        in_specs=[whole] * 3,
        out_specs=[whole] * 2,
        scratch_shapes=[
            vmem((HEADS, WIDTH, TOK), BF16),
            vmem((N_TP, PIECE, TOK), BF16),
            vmem((1, TOK), I32),
            vmem((WIDTH, TOK), BF16),
            dma((HEADS + 2,)),
            dma((HEADS + 1,)),
        ],
        compiler_params=pltpu.CompilerParams(vmem_limit_bytes=63 << 20),
        name="finish",
    )(d_query, pieces, here)
    return (d_query.transpose(2, 0, 1), d_latent.T)


def solution(mesh):
    return jax.shard_map(
        local,
        mesh=mesh,
        in_specs=(P("ctx", "tp", None), P("ctx", None), P("ctx", "tp", None), P("ctx"), P()),
        out_specs=(P("ctx", "tp", None), P("ctx", None)),
        check_vma=False,
    )
```
